32 devices in a mesh: row: 8 (over y, x, core), col: 4 (over z).
Axes of the slice: x: 2, y: 2, z: 4, core: 2. Of those that a mesh axis runs over, the one named last changes fastest.
Arguments:
- features: bfloat16 [12, 8, 128, 512], P(None, 'row', 'col'), may hold values from -6 to 6
Outputs:
- panels: float32 [12, 8, 128, 256], P(None, 'row')
- trailing: float32 [12, 8, 128, 24, 4, 128], P(None, 'row', None, None, 'col')
The draws below stay inside these ranges and needn't reach their ends.
All inputs are finite; a program needn't handle non-finite values.
Results may differ from the reference program's by a relative error of at most 0.0003.
Values may be sent and summed in bfloat16 or wider, within the bound.
No kernel may reach another device: no remote copies, remote signals or barrier semaphores. Data moves between devices by JAX's collectives and lax.ppermute only.
A program may use at most 128 MiB of HBM per device.

```python
import math
import jax
import jax.numpy as jnp
from jax import lax

N = 12288
F = 512
TILE = 128
PANEL = 256
PANELS = 1
LAYERS = 2
RT = 12
CT = 24
N_ROW = 8
N_COL = 4


def steps_of(stream_key, dims, pieces, low, top_value):
    factor_of = 1.0
    for position, shards_of in pieces:
        steps = jax.random.uniform(jax.random.fold_in(jax.random.fold_in(stream_key, 6), position), (shards_of,), jnp.float32, low / len(pieces), top_value / len(pieces))
        factor_of = factor_of * jnp.repeat(jnp.exp(steps), dims[position] // shards_of).reshape((-1,) + (1,) * (len(dims) - 1 - position))
    return factor_of


def scatter_about(rng, extent, spread, reach, cuts=(), held_as=jnp.bfloat16):
    values = spread * jax.random.normal(rng, extent, jnp.float32)
    if cuts:
        values = values * steps_of(rng, extent, cuts, -0.22, 0.18)
    return jnp.clip(values, -reach, reach).astype(held_as)


def setup_inputs(seed: int = 0) -> dict:
    arg_keys = jax.random.split(jax.random.key(seed), 2)
    features = scatter_about(arg_keys[0], (RT, N_ROW, TILE, F), 1.0, 6.0, ((1, 8), (2, 4)))
    return {"features": features}


def kernel_rows(x_rows, q_rows, x_all, q_all, row_ids, col_ids):
    gram = jnp.dot(x_rows.astype(jnp.float32), x_all.T.astype(jnp.float32), preferred_element_type=jnp.float32) / F
    scale = jnp.sqrt(q_rows[:, None] * q_all[None, :])
    same = row_ids[:, None] == col_ids[None, :]
    rho = jnp.where(same, 1.0, gram / scale)
    theta = gram
    for layer in range(LAYERS):
        angle = jnp.arccos(rho)
        jfun = (jnp.sqrt(1.0 - rho * rho) + (math.pi - angle) * rho) / math.pi
        theta = theta * (math.pi - angle) / math.pi + scale * jfun
        rho = jfun
    return theta + jnp.where(same, 1.0, 0.0)

def reference(features):
    x_all = features.reshape(N, F)
    q_all = lax.optimization_barrier(jnp.sum(x_all.astype(jnp.float32) ** 2, axis=1)) / F + 1e-06
    col_ids = jnp.arange(N, dtype=jnp.int32)
    block = 1024 if N % 1024 == 0 else N
    starts = jnp.arange(N // block, dtype=jnp.int32) * block

    def one_block(start):
        xs = lax.dynamic_slice_in_dim(x_all, start, block, 0)
        qs = lax.dynamic_slice_in_dim(q_all, start, block, 0)
        ids = start + jnp.arange(block, dtype=jnp.int32)
        return kernel_rows(xs, qs, x_all, q_all, ids, col_ids)
    kmat = lax.map(one_block, starts).reshape(N, N)
    outs = []
    for panel in range(PANELS):
        lo = panel * PANEL
        chol = jnp.linalg.cholesky(kmat[lo:lo + PANEL, lo:lo + PANEL])
        lower = lax.linalg.triangular_solve(chol, kmat[:, lo:lo + PANEL], left_side=False, lower=True, transpose_a=True)
        lower = jnp.where(col_ids[:, None] < lo, 0.0, lower)
        kmat = kmat - jnp.dot(lower, lower.T, precision=lax.Precision.HIGHEST)
        outs.append(lower)
    panels = jnp.concatenate(outs, axis=1).reshape(RT, N_ROW, TILE, PANELS * PANEL)
    return (panels, kmat.reshape(RT, N_ROW, TILE, CT, N_COL, TILE))
```

```python
import functools

import jax
import jax.numpy as jnp
from jax import lax
from jax.experimental import pallas as pl
from jax.experimental.pallas import tpu as pltpu
from jax.sharding import PartitionSpec as P

F = 512
PANEL = 256
TILE = 128
RIDGE = 1.0
EPS = 1e-6

PV = (-2.265364170074463, -4.70527982711792, 7.536093711853027,
      0.7343835830688477, -1.7677195072174072, 0.3254770040512085)
QV = (1.8269329071044922, 3.1679749488830566, -4.871670722961426,
      0.626383364200592, 0.07849788665771484)
TINY = 1e-30
NT = (((1,), (1,)), ((), ()))
VMEM_LIMIT = 60 * 2**20


def dot_nt(a, b):
    return lax.dot_general(a, b, NT, preferred_element_type=jnp.float32)


def dot_hi(a, b, dims):
    return lax.dot_general(
        a, b, (dims, ((), ())), precision=lax.Precision.HIGHEST,
        preferred_element_type=jnp.float32,
    )


def horner(x, coefs):
    acc = coefs[-1]
    for c in coefs[-2::-1]:
        acc = acc * x + c
    return acc


def two_layers(rho):
    a = jnp.maximum(1.0 - rho, TINY)
    b = jnp.maximum(1.0 + rho, TINY)
    u = a * lax.rsqrt(a)
    v = b * lax.rsqrt(b)
    return horner(v, PV) + u * horner(v, QV)


def norm_rows(x):
    xf = x.astype(jnp.float32)
    return jnp.sum(xf * xf, axis=1, keepdims=True) / F


def norm_lanes(x):
    xf = x.astype(jnp.float32)
    sq = xf * xf
    hi = sq.astype(jnp.bfloat16)
    lo = (sq - hi.astype(jnp.float32)).astype(jnp.bfloat16)
    ones = jnp.ones((8, x.shape[1]), jnp.bfloat16)
    return (dot_nt(ones, hi) + dot_nt(ones, lo)) / F


def eye(n):
    return lax.broadcasted_iota(jnp.int32, (n, n), 0) == lax.broadcasted_iota(
        jnp.int32, (n, n), 1
    )


def eliminate(w_ref, t_ref):
    n = TILE
    sub = lax.broadcasted_iota(jnp.int32, (8, n), 0)
    for p in range(0, n, 8):
        a8 = w_ref[p : p + 8, :n]
        e8 = w_ref[p : p + 8, n:]
        cols = [jnp.broadcast_to(a8[:, p + k : p + k + 1], (8, n)) for k in range(8)]
        root = jnp.ones((8, n), jnp.float32)
        invs, ups = [], []
        for k in range(8):
            piv = cols[k][k : k + 1, :]
            inv = 1.0 / piv
            m = jnp.where(sub > k, cols[k] * inv, 0.0)
            ak, ek = a8[k : k + 1, :], e8[k : k + 1, :]
            up = [cols[j][k : k + 1, :] for j in range(k + 1, 8)]
            for j in range(k + 1, 8):
                cols[j] = cols[j] - m * up[j - k - 1]
            a8 = a8 - m * ak
            e8 = e8 - m * ek
            root = jnp.where(sub == k, lax.rsqrt(piv), root)
            invs.append(inv)
            ups.append((ak, ek, up))
        t_ref[p : p + 8, :] = e8 * root
        for g in range(p + 8, n, 8):
            a = w_ref[g : g + 8, :n]
            e = w_ref[g : g + 8, n:]
            cs = [jnp.broadcast_to(a[:, p + k : p + k + 1], (8, n)) for k in range(8)]
            for k in range(8):
                ak, ek, up = ups[k]
                m = cs[k] * invs[k]
                for j in range(k + 1, 8):
                    cs[j] = cs[j] - m * up[j - k - 1]
                a = a - m * ak
                e = e - m * ek
            w_ref[g : g + 8, :n] = a
            w_ref[g : g + 8, n:] = e


def factor_kernel(x_ref, t_ref, sp_ref, bp_ref, k_ref, w_ref, t1_ref, t2_ref):
    x = x_ref[...]
    gq_l = norm_lanes(x)
    s_l = jnp.sqrt(gq_l + EPS)
    b_l = 1.0 / s_l
    sp_ref[...] = s_l
    bp_ref[...] = b_l
    gq = norm_rows(x)
    s = jnp.sqrt(gq + EPS)
    rho = dot_nt(x, x) * ((1.0 / F) / s) * b_l[0:1, :]
    k = two_layers(rho) * (s * s_l[0:1, :])
    k_ref[...] = jnp.where(eye(PANEL), 3.0 * gq + (2.0 * EPS + RIDGE), k)
    h = PANEL // 2
    ident = jnp.where(eye(h), 1.0, 0.0)
    w_ref[:, :h] = k_ref[:h, :h]
    w_ref[:, h:] = ident
    eliminate(w_ref, t1_ref)
    t1 = t1_ref[...]
    l21 = dot_hi(k_ref[h:, :h], t1, ((1,), (1,)))
    w_ref[:, :h] = k_ref[h:, h:] - dot_hi(l21, l21, ((1,), (1,)))
    w_ref[:, h:] = ident
    eliminate(w_ref, t2_ref)
    t2 = t2_ref[...]
    t_ref[:h, :h] = t1
    t_ref[:h, h:] = jnp.zeros((h, h), jnp.float32)
    t_ref[h:, :h] = -dot_hi(t2, dot_hi(l21, t1, ((1,), (0,))), ((1,), (0,)))
    t_ref[h:, h:] = t2


def factor(points):
    full = jax.ShapeDtypeStruct((PANEL, PANEL), jnp.float32)
    vec = jax.ShapeDtypeStruct((8, PANEL), jnp.float32)
    return pl.pallas_call(
        factor_kernel,
        out_shape=[full, vec, vec],
        scratch_shapes=[
            pltpu.VMEM((PANEL, PANEL), jnp.float32),
            pltpu.VMEM((TILE, 2 * TILE), jnp.float32),
            pltpu.VMEM((TILE, TILE), jnp.float32),
            pltpu.VMEM((TILE, TILE), jnp.float32),
        ],
        compiler_params=pltpu.CompilerParams(vmem_limit_bytes=VMEM_LIMIT),
        cost_estimate=pl.CostEstimate(flops=10**9, bytes_accessed=10**7, transcendentals=0),
        name="factor",
    )(points)


def panel_kernel(is_rows, block, tau_ref, x_ref, pts_ref, t_ref, sp_ref, bp_ref, *refs):
    outs, k_ref = refs[:-1], refs[-1]
    x = x_ref[...]
    gq = norm_rows(x)
    s = jnp.sqrt(gq + EPS)
    a = (1.0 / F) / s
    diag = 3.0 * gq + (2.0 * EPS + RIDGE)
    k_ref[...] = dot_nt(x, pts_ref[...])
    sp = sp_ref[0:1, :]
    bp = bp_ref[0:1, :]
    for g in range(0, block, 16):
        rows = slice(g, g + 16)
        rho = k_ref[rows, :] * a[rows, :] * bp
        k_ref[rows, :] = two_layers(rho) * (s[rows, :] * sp)
    for half in range(PANEL // TILE):

        @pl.when((pl.program_id(0) == 0) & (tau_ref[0] == half))
        def _():
            cols = slice(half * TILE, (half + 1) * TILE)
            k_ref[:TILE, cols] = jnp.where(eye(TILE), diag[:TILE, :], k_ref[:TILE, cols])

    low = dot_hi(k_ref[...], t_ref[...], ((1,), (1,)))
    hi = low.astype(jnp.bfloat16)
    lo = (low - hi.astype(jnp.float32)).astype(jnp.bfloat16)
    if is_rows:
        l_ref, cat_ref, s_ref, a_ref, d_ref = outs
        l_ref[...] = low
        cat_ref[:, :PANEL] = hi
        cat_ref[:, PANEL : 2 * PANEL] = hi
        cat_ref[:, 2 * PANEL :] = lo
        s_ref[...] = jnp.broadcast_to(s, s_ref.shape)
        a_ref[...] = jnp.broadcast_to(a, a_ref.shape)
        left = diag - jnp.sum(low * low, axis=1, keepdims=True)
        d_ref[...] = jnp.broadcast_to(left, d_ref.shape)
    else:
        cat_ref, s_ref, b_ref = outs
        cat_ref[:, :PANEL] = hi
        cat_ref[:, PANEL : 2 * PANEL] = lo
        cat_ref[:, 2 * PANEL :] = hi
        s_l = jnp.sqrt(norm_lanes(x) + EPS)
        s_ref[...] = s_l
        b_ref[...] = 1.0 / s_l


def pick(total, options):
    for o in options:
        if total % o == 0:
            return o
    return total


def panel(is_rows, x, points, t, sp, bp, tau):
    m = x.shape[0]
    block = pick(m, (512, 384, 256, 128))
    const = lambda shape: pl.BlockSpec(shape, lambda i: (0, 0))
    by_row = lambda width: pl.BlockSpec((block, width), lambda i: (i, 0))
    by_lane = pl.BlockSpec((8, block), lambda i: (0, i))
    f32 = lambda *shape: jax.ShapeDtypeStruct(shape, jnp.float32)
    cat = jax.ShapeDtypeStruct((m, 3 * PANEL), jnp.bfloat16)
    if is_rows:
        shapes = [f32(m, PANEL), cat, f32(m, 128), f32(m, 128), f32(m, 128)]
        specs = [by_row(PANEL), by_row(3 * PANEL)] + [by_row(128)] * 3
    else:
        shapes = [cat, f32(8, m), f32(8, m)]
        specs = [by_row(3 * PANEL), by_lane, by_lane]
    return pl.pallas_call(
        functools.partial(panel_kernel, is_rows, block),
        grid=(m // block,),
        in_specs=[
            pl.BlockSpec(memory_space=pltpu.SMEM),
            by_row(F), const((PANEL, F)), const((PANEL, PANEL)),
            const((8, PANEL)), const((8, PANEL)),
        ],
        out_specs=specs,
        out_shape=shapes,
        scratch_shapes=[pltpu.VMEM((block, PANEL), jnp.float32)],
        compiler_params=pltpu.CompilerParams(vmem_limit_bytes=VMEM_LIMIT),
        cost_estimate=pl.CostEstimate(
            flops=2 * m * PANEL * (F + 6 * PANEL), bytes_accessed=m * 4096, transcendentals=0
        ),
        name="panel_rows" if is_rows else "panel_cols",
    )(tau, x, points, t, sp, bp)


def trailing_kernel(rb, cb, tb, steps, step_tiles, diag_ref, xr, xc, lr, lc, sr, ar, dr, sc, bc,
                    out, ga, ma, gb, mb):
    i = pl.program_id(0)
    r0 = pl.multiple_of(i * rb, rb)
    per = cb // TILE
    chunks = tb // per

    def multiply(row, col, g, m):
        g[...] = dot_nt(xr[pl.ds(row, rb), :], xc[pl.ds(col, cb), :])
        m[...] = dot_nt(lr[pl.ds(row, rb), :], lc[pl.ds(col, cb), :])

    def finish(n, g, m):
        for t in range(per):
            lanes = pl.ds(pl.multiple_of(n * cb + t * TILE, TILE), TILE)
            s_col = sc[0:1, lanes]
            b_col = bc[0:1, lanes]
            here = slice(t * TILE, (t + 1) * TILE)
            for k in range(0, rb, 16):
                rows = pl.ds(r0 + k, 16)
                rho = g[k : k + 16, here] * ar[rows, :] * b_col
                val = two_layers(rho) * (sr[rows, :] * s_col) - m[k : k + 16, here]
                out[pl.ds(k * tb + n * per + t, 16, stride=tb), :] = val

    @pl.when(i == 0)
    def _():
        multiply(0, 0, ga, ma)

    @pl.loop(0, chunks // 2)
    def _(h):
        n = 2 * h
        multiply(r0, pl.multiple_of((n + 1) * cb, cb), gb, mb)
        finish(n, ga, ma)
        last = n + 2 >= chunks
        row = jnp.where(last, jnp.minimum(i + 1, steps - 1) * rb, r0)
        col = jnp.where(last, 0, (n + 2) * cb)
        multiply(pl.multiple_of(row, rb), pl.multiple_of(col, cb), ga, ma)
        finish(n + 1, gb, mb)

    @pl.when(diag_ref[0] == 1)
    def _():
        for tile in range(rb // TILE):
            col = (i * (rb // TILE) + tile) * step_tiles + diag_ref[1]
            for k in range(0, TILE, 16):
                rows = pl.ds(r0 + tile * TILE + k, 16)
                same = lax.broadcasted_iota(jnp.int32, (16, TILE), 1) == (
                    lax.broadcasted_iota(jnp.int32, (16, TILE), 0) + k
                )
                at = pl.ds((tile * TILE + k) * tb + col, 16, stride=tb)
                out[at, :] = jnp.where(same, dr[rows, :], out[at, :])


def trailing(x_rows, x_cols, cat_rows, cat_cols, s, a, d, sc, bc, diag, step_tiles):
    m, n = x_rows.shape[0], x_cols.shape[0]
    tb = n // TILE
    rb = pick(m, (512, 384, 256, 128))
    cb = 2 * TILE if (tb // 2) % 2 == 0 and tb % 2 == 0 else TILE
    const = lambda shape: pl.BlockSpec(shape, lambda i: (0, 0))
    return pl.pallas_call(
        functools.partial(trailing_kernel, rb, cb, tb, m // rb, step_tiles),
        grid=(m // rb,),
        in_specs=[
            pl.BlockSpec(memory_space=pltpu.SMEM),
            const((m, F)), const((n, F)), const((m, 3 * PANEL)), const((n, 3 * PANEL)),
            const((m, 128)), const((m, 128)), const((m, 128)), const((8, n)), const((8, n)),
        ],
        out_specs=pl.BlockSpec((rb * tb, TILE), lambda i: (i, 0)),
        out_shape=jax.ShapeDtypeStruct((m * tb, TILE), jnp.float32),
        scratch_shapes=[pltpu.VMEM((rb, cb), jnp.float32)] * 4,
        compiler_params=pltpu.CompilerParams(vmem_limit_bytes=VMEM_LIMIT),
        cost_estimate=pl.CostEstimate(
            flops=2 * m * n * (F + 3 * PANEL), bytes_accessed=m * n * 4, transcendentals=0
        ),
        name="trailing",
    )(diag, x_rows, x_cols, cat_rows, cat_cols, s, a, d, sc, bc)


def spread(data, n_row, n_col, r, c):
    low = n_col.bit_length() - 1
    high = n_row.bit_length() - 1

    def send(value, bit, mask):
        pairs = [
            (i * n_col + j, (i ^ (1 << bit)) * n_col + j)
            for i in range(n_row) for j in range(n_col) if (i ^ j) & mask == 0
        ]
        return lax.ppermute(value, ("row", "col"), pairs)

    mask = n_col - 1
    for bit in range(low - 1, 0, -1):
        got = send(data, bit, mask)
        mask &= ~(1 << bit)
        data = jnp.where(((r ^ c) >> bit) & 1 == 0, data, got)
    parts = data[None]
    for bit in range(low, high):
        got = send(parts, bit, mask)
        first = (r >> bit) & 1 == 0
        parts = jnp.concatenate([jnp.where(first, parts, got), jnp.where(first, got, parts)])
    if low > 0:
        got = send(parts, 0, mask)
        parts = jnp.where((r ^ c) & 1 == 0, parts, got)
    return parts


def local(features):
    n_row, n_col = lax.axis_size("row"), lax.axis_size("col")
    r, c = lax.axis_index("row"), lax.axis_index("col")
    tiles_r, _, thin, width = features.shape
    step_tiles = n_row // n_col
    tiles_c = tiles_r * step_tiles
    tile = thin * n_col

    points = lax.all_gather(features[0, 0], "row", axis=0)[: PANEL // tile]
    points = lax.all_gather(points, "col", axis=1, tiled=True).reshape(PANEL, width)
    t, sp, bp = factor(points)

    row_feat = lax.all_gather(features, "col", axis=2, tiled=True).reshape(tiles_r, tile, width)
    x_rows = row_feat.reshape(tiles_r * tile, width)
    col_feat = spread(row_feat, n_row, n_col, r, c)
    x_cols = jnp.swapaxes(col_feat, 0, 1).reshape(tiles_c * tile, width)

    tau = lambda i: jnp.where(i < PANEL // tile, i, -1).astype(jnp.int32).reshape(1)
    low, cat_rows, s, a, d = panel(True, x_rows, points, t, sp, bp, tau(r))
    cat_cols, sc, bc = panel(False, x_cols, points, t, sp, bp, tau(c))
    on_diag = ((r - c) % n_col == 0).astype(jnp.int32)
    diag = jnp.stack([on_diag, (r - c) // n_col]).astype(jnp.int32)
    out = trailing(x_rows, x_cols, cat_rows, cat_cols, s, a, d, sc, bc, diag, step_tiles)
    return (
        low.reshape(tiles_r, 1, tile, PANEL),
        out.reshape(tiles_r, 1, tile, tiles_c, 1, tile),
    )


def solution(mesh):
    return jax.shard_map(
        local,
        mesh=mesh,
        in_specs=(P(None, "row", "col", None),),
        out_specs=(P(None, "row", None, None), P(None, "row", None, None, "col", None)),
        check_vma=False,
    )
```

```python
import functools

import jax
import jax.numpy as jnp
from jax import lax
from jax.experimental import pallas as pl
from jax.experimental.pallas import tpu as pltpu
from jax.sharding import PartitionSpec as P

F = 512
PANEL = 256
TILE = 128
RIDGE = 1.0
EPS = 1e-6

PV = (-2.265364170074463, -4.70527982711792, 7.536093711853027,
      0.7343835830688477, -1.7677195072174072, 0.3254770040512085)
QV = (1.8269329071044922, 3.1679749488830566, -4.871670722961426,
      0.626383364200592, 0.07849788665771484)
TINY = 1e-30
NT = (((1,), (1,)), ((), ()))
VMEM_LIMIT = 60 * 2**20


def dot_nt(a, b):
    return lax.dot_general(a, b, NT, preferred_element_type=jnp.float32)


def dot_hi(a, b, dims):
    return lax.dot_general(
        a, b, (dims, ((), ())), precision=lax.Precision.HIGHEST,
        preferred_element_type=jnp.float32,
    )


def horner(x, coefs):
    acc = coefs[-1]
    for c in coefs[-2::-1]:
        acc = acc * x + c
    return acc


def two_layers(rho):
    a = jnp.maximum(1.0 - rho, TINY)
    b = jnp.maximum(1.0 + rho, TINY)
    u = a * lax.rsqrt(a)
    v = b * lax.rsqrt(b)
    return horner(v, PV) + u * horner(v, QV)


def norm_rows(x):
    xf = x.astype(jnp.float32)
    return jnp.sum(xf * xf, axis=1, keepdims=True) / F


def norm_lanes(x):
    xf = x.astype(jnp.float32)
    sq = xf * xf
    hi = sq.astype(jnp.bfloat16)
    lo = (sq - hi.astype(jnp.float32)).astype(jnp.bfloat16)
    ones = jnp.ones((8, x.shape[1]), jnp.bfloat16)
    return (dot_nt(ones, hi) + dot_nt(ones, lo)) / F


def eye(n):
    return lax.broadcasted_iota(jnp.int32, (n, n), 0) == lax.broadcasted_iota(
        jnp.int32, (n, n), 1
    )


def eliminate(w_ref, t_ref):
    n = TILE
    sub = lax.broadcasted_iota(jnp.int32, (8, n), 0)
    for p in range(0, n, 8):
        a8 = w_ref[p : p + 8, :n]
        e8 = w_ref[p : p + 8, n:]
        cols = [jnp.broadcast_to(a8[:, p + k : p + k + 1], (8, n)) for k in range(8)]
        root = jnp.ones((8, n), jnp.float32)
        invs, ups = [], []
        for k in range(8):
            piv = cols[k][k : k + 1, :]
            inv = 1.0 / piv
            m = jnp.where(sub > k, cols[k] * inv, 0.0)
            ak, ek = a8[k : k + 1, :], e8[k : k + 1, :]
            up = [cols[j][k : k + 1, :] for j in range(k + 1, 8)]
            for j in range(k + 1, 8):
                cols[j] = cols[j] - m * up[j - k - 1]
            a8 = a8 - m * ak
            e8 = e8 - m * ek
            root = jnp.where(sub == k, lax.rsqrt(piv), root)
            invs.append(inv)
            ups.append((ak, ek, up))
        t_ref[p : p + 8, :] = e8 * root
        for g in range(p + 8, n, 8):
            a = w_ref[g : g + 8, :n]
            e = w_ref[g : g + 8, n:]
            cs = [jnp.broadcast_to(a[:, p + k : p + k + 1], (8, n)) for k in range(8)]
            for k in range(8):
                ak, ek, up = ups[k]
                m = cs[k] * invs[k]
                for j in range(k + 1, 8):
                    cs[j] = cs[j] - m * up[j - k - 1]
                a = a - m * ak
                e = e - m * ek
            w_ref[g : g + 8, :n] = a
            w_ref[g : g + 8, n:] = e


def factor_kernel(x_ref, t_ref, sp_ref, bp_ref, k_ref, w_ref, t1_ref, t2_ref):
    x = x_ref[...]
    gq_l = norm_lanes(x)
    s_l = jnp.sqrt(gq_l + EPS)
    b_l = 1.0 / s_l
    sp_ref[...] = s_l
    bp_ref[...] = b_l
    gq = norm_rows(x)
    s = jnp.sqrt(gq + EPS)
    rho = dot_nt(x, x) * ((1.0 / F) / s) * b_l[0:1, :]
    k = two_layers(rho) * (s * s_l[0:1, :])
    k_ref[...] = jnp.where(eye(PANEL), 3.0 * gq + (2.0 * EPS + RIDGE), k)
    h = PANEL // 2
    ident = jnp.where(eye(h), 1.0, 0.0)
    w_ref[:, :h] = k_ref[:h, :h]
    w_ref[:, h:] = ident
    eliminate(w_ref, t1_ref)
    t1 = t1_ref[...]
    l21 = dot_hi(k_ref[h:, :h], t1, ((1,), (1,)))
    w_ref[:, :h] = k_ref[h:, h:] - dot_hi(l21, l21, ((1,), (1,)))
    w_ref[:, h:] = ident
    eliminate(w_ref, t2_ref)
    t2 = t2_ref[...]
    t_ref[:h, :h] = t1
    t_ref[:h, h:] = jnp.zeros((h, h), jnp.float32)
    t_ref[h:, :h] = -dot_hi(t2, dot_hi(l21, t1, ((1,), (0,))), ((1,), (0,)))
    t_ref[h:, h:] = t2


def factor(points):
    full = jax.ShapeDtypeStruct((PANEL, PANEL), jnp.float32)
    vec = jax.ShapeDtypeStruct((8, PANEL), jnp.float32)
    return pl.pallas_call(
        factor_kernel,
        out_shape=[full, vec, vec],
        scratch_shapes=[
            pltpu.VMEM((PANEL, PANEL), jnp.float32),
            pltpu.VMEM((TILE, 2 * TILE), jnp.float32),
            pltpu.VMEM((TILE, TILE), jnp.float32),
            pltpu.VMEM((TILE, TILE), jnp.float32),
        ],
        compiler_params=pltpu.CompilerParams(vmem_limit_bytes=VMEM_LIMIT),
        cost_estimate=pl.CostEstimate(flops=10**9, bytes_accessed=10**7, transcendentals=0),
        name="factor",
    )(points)


def panel_block(x, pts, sp, bp, k_ref):
    gq = norm_rows(x)
    s = jnp.sqrt(gq + EPS)
    a = (1.0 / F) / s
    k_ref[...] = dot_nt(x, pts)
    for g in range(0, x.shape[0], 16):
        rows = slice(g, g + 16)
        rho = k_ref[rows, :] * a[rows, :] * bp
        k_ref[rows, :] = two_layers(rho) * (s[rows, :] * sp)
    return s, a, 3.0 * gq + (2.0 * EPS + RIDGE)


def set_diagonal(k_ref, diag, hit):
    for half in range(PANEL // TILE):

        @pl.when(hit == half)
        def _():
            cols = slice(half * TILE, (half + 1) * TILE)
            k_ref[:TILE, cols] = jnp.where(eye(TILE), diag[:TILE, :], k_ref[:TILE, cols])


def split(low):
    hi = low.astype(jnp.bfloat16)
    return hi, (low - hi.astype(jnp.float32)).astype(jnp.bfloat16)


def panel_kernel(tau_ref, x_ref, pts_ref, t_ref, sp_ref, bp_ref,
                 l_ref, cat_ref, s_ref, a_ref, d_ref, k_ref):
    s, a, diag = panel_block(x_ref[...], pts_ref[...], sp_ref[0:1, :], bp_ref[0:1, :], k_ref)
    set_diagonal(k_ref, diag, jnp.where(pl.program_id(0) == 0, tau_ref[0], -1))
    low = dot_hi(k_ref[...], t_ref[...], ((1,), (1,)))
    hi, lo = split(low)
    l_ref[...] = low
    cat_ref[:, :PANEL] = hi
    cat_ref[:, PANEL : 2 * PANEL] = hi
    cat_ref[:, 2 * PANEL :] = lo
    s_ref[...] = jnp.broadcast_to(s, s_ref.shape)
    a_ref[...] = jnp.broadcast_to(a, a_ref.shape)
    left = diag - jnp.sum(low * low, axis=1, keepdims=True)
    d_ref[...] = jnp.broadcast_to(left, d_ref.shape)


def pick(total, options):
    for o in options:
        if total % o == 0:
            return o
    return total


def panel_rows(x, points, t, sp, bp, tau):
    m = x.shape[0]
    block = pick(m, (512, 384, 256, 128))
    const = lambda shape: pl.BlockSpec(shape, lambda i: (0, 0))
    by_row = lambda width: pl.BlockSpec((block, width), lambda i: (i, 0))
    f32 = lambda *shape: jax.ShapeDtypeStruct(shape, jnp.float32)
    return pl.pallas_call(
        panel_kernel,
        grid=(m // block,),
        in_specs=[
            pl.BlockSpec(memory_space=pltpu.SMEM),
            by_row(F), const((PANEL, F)), const((PANEL, PANEL)),
            const((8, PANEL)), const((8, PANEL)),
        ],
        out_specs=[by_row(PANEL), by_row(3 * PANEL)] + [by_row(128)] * 3,
        out_shape=[f32(m, PANEL), jax.ShapeDtypeStruct((m, 3 * PANEL), jnp.bfloat16),
                   f32(m, 128), f32(m, 128), f32(m, 128)],
        scratch_shapes=[pltpu.VMEM((block, PANEL), jnp.float32)],
        compiler_params=pltpu.CompilerParams(vmem_limit_bytes=VMEM_LIMIT),
        cost_estimate=pl.CostEstimate(
            flops=2 * m * PANEL * (F + 6 * PANEL), bytes_accessed=m * 4096, transcendentals=0
        ),
        name="panel_rows",
    )(tau, x, points, t, sp, bp)


def trailing_kernel(rb, tb, blocks, steps, step_tiles, fold, arrays, info, *refs):
    mine, got, refs = refs[:arrays], refs[arrays : 2 * arrays], refs[2 * arrays :]
    pts, t_ref, sp_ref, bp_ref, xr, xr_next, lr, lr_next, sr, ar, dr = refs[:11]
    out, xc, lc, sc, bc, k_ref, ga, ma, gb, mb, sem = refs[-11:]
    if fold:
        out = out.reshape(rb * tb, TILE)
    q = pl.program_id(0)
    i, j = q // blocks, q % blocks
    cb = tb * TILE // 2
    per = cb // TILE

    def load(arrays):
        moves = []
        for k, src in enumerate(arrays):
            group, entry = k // step_tiles, k % step_tiles
            part = info[4] ^ entry
            width = src.shape[1]

            def move(tile):
                at = (tile * step_tiles + part) * TILE + info[5 + group] * width
                to = pl.ds(pl.multiple_of(at, width), width)
                return pltpu.make_async_copy(src.at[tile], xc.at[to], sem)

            for tile in range(src.shape[0]):
                moves.append(move(tile))
        for m in moves:
            m.start()
        for m in moves:
            m.wait()

    def columns(b):
        size = k_ref.shape[0]
        rows = pl.ds(pl.multiple_of(b * size, size), size)
        s, _, diag = panel_block(xc[rows, :], pts[...], sp_ref[0:1, :], bp_ref[0:1, :], k_ref)
        set_diagonal(k_ref, diag, jnp.where(b == 0, info[2], -1))
        hi, lo = split(dot_hi(k_ref[...], t_ref[...], ((1,), (1,))))
        lc[rows, :PANEL] = hi
        lc[rows, PANEL : 2 * PANEL] = lo
        lc[rows, 2 * PANEL :] = hi
        for g in range(0, size, TILE):
            wide = jnp.broadcast_to(s[g : g + TILE, :], (TILE, TILE)).T[0:8, :]
            lanes = pl.ds(pl.multiple_of(b * size + g, TILE), TILE)
            sc[:, lanes] = wide
            bc[:, lanes] = 1.0 / wide

    def multiply(x, l, col, g, m):
        cols = pl.ds(pl.multiple_of(col, cb), cb)
        g[...] = dot_nt(x[...], xc[cols, :])
        m[...] = dot_nt(l[...], lc[cols, :])

    def finish(half, g, m):
        for tile in range(per):
            lanes = pl.ds(pl.multiple_of(j * (tb * TILE) + half * cb + tile * TILE, TILE), TILE)
            s_col = sc[0:1, lanes]
            b_col = bc[0:1, lanes]
            here = slice(tile * TILE, (tile + 1) * TILE)
            for k in range(0, rb, 16):
                rows = slice(k, k + 16)
                rho = g[rows, here] * ar[rows, :] * b_col
                val = two_layers(rho) * (sr[rows, :] * s_col) - m[rows, here]
                out[pl.ds(k * tb + half * per + tile, 16, stride=tb), :] = val

    @pl.when(q == 0)
    def _():
        @pl.when(info[3] == 0)
        def _():
            load(mine)

        @pl.when(info[3] != 0)
        def _():
            load(got)

        @pl.loop(0, xc.shape[0] // k_ref.shape[0])
        def _(b):
            columns(b)

        multiply(xr, lr, 0, ga, ma)

    multiply(xr, lr, j * (tb * TILE) + cb, gb, mb)
    finish(0, ga, ma)
    after = jnp.minimum(q + 1, steps - 1) % blocks
    multiply(xr_next, lr_next, after * (tb * TILE), ga, ma)
    finish(1, gb, mb)

    for tile in range(rb // TILE):
        col = (i * (rb // TILE) + tile) * step_tiles + info[1] - j * tb

        @pl.when((info[0] == 1) & (col >= 0) & (col < tb))
        def _():
            for k in range(0, TILE, 16):
                rows = slice(tile * TILE + k, tile * TILE + k + 16)
                same = lax.broadcasted_iota(jnp.int32, (16, TILE), 1) == (
                    lax.broadcasted_iota(jnp.int32, (16, TILE), 0) + k
                )
                at = pl.ds((tile * TILE + k) * tb + col, 16, stride=tb)
                out[at, :] = jnp.where(same, dr[rows, :], out[at, :])


def trailing(row_args, mine, got, panel_args, info, step_tiles):
    x_rows, cat_rows, s, a, d = row_args
    m = x_rows.shape[0]
    tiles_c = m // TILE * step_tiles
    n = tiles_c * TILE
    fold = tiles_c % 8 == 0
    tb = 8 if fold else tiles_c
    rb = pick(m, (512, 384, 256, 128))
    cb = tb * TILE // 2
    blocks = n // (tb * TILE)
    steps = m // rb * blocks
    const = lambda shape: pl.BlockSpec(shape, lambda q: (0, 0))
    cur = lambda width: pl.BlockSpec((rb, width), lambda q: (q // blocks, 0))
    nxt = lambda width: pl.BlockSpec(
        (rb, width), lambda q: (jnp.minimum(q + 1, steps - 1) // blocks, 0)
    )
    hbm = pl.BlockSpec(memory_space=pl.ANY)
    if fold:
        shape = (m, tiles_c, TILE)
        spec = pl.BlockSpec((rb, tb, TILE), lambda q: (q // blocks, q % blocks, 0))
    else:
        shape = (m * tb, TILE)
        spec = pl.BlockSpec((rb * tb, TILE), lambda q: (q, 0))
    square = pltpu.VMEM((rb, cb), jnp.float32)
    return pl.pallas_call(
        functools.partial(
            trailing_kernel, rb, tb, blocks, steps, step_tiles, fold, len(mine)
        ),
        grid=(steps,),
        in_specs=[pl.BlockSpec(memory_space=pltpu.SMEM)] + [hbm] * (2 * len(mine)) + [
            const((PANEL, F)), const((PANEL, PANEL)), const((8, PANEL)), const((8, PANEL)),
            cur(F), nxt(F), cur(3 * PANEL), nxt(3 * PANEL), cur(128), cur(128), cur(128),
        ],
        out_specs=spec,
        out_shape=jax.ShapeDtypeStruct(shape, jnp.float32),
        scratch_shapes=[
            pltpu.VMEM((n, F), jnp.bfloat16),
            pltpu.VMEM((n, 3 * PANEL), jnp.bfloat16),
            pltpu.VMEM((8, n), jnp.float32),
            pltpu.VMEM((8, n), jnp.float32),
            pltpu.VMEM((pick(n, (512, 384, 256, 128)), PANEL), jnp.float32),
            square, square, square, square,
            pltpu.SemaphoreType.DMA,
        ],
        compiler_params=pltpu.CompilerParams(vmem_limit_bytes=VMEM_LIMIT),
        cost_estimate=pl.CostEstimate(
            flops=2 * m * n * (F + 3 * PANEL), bytes_accessed=m * n * 4, transcendentals=0
        ),
        name="trailing",
    )(info, *mine, *got, *panel_args, x_rows, x_rows, cat_rows, cat_rows, s, a, d)


class Grid:
    def __init__(self):
        self.n_row, self.n_col = lax.axis_size("row"), lax.axis_size("col")
        self.r, self.c = lax.axis_index("row"), lax.axis_index("col")
        self.low = self.n_col.bit_length() - 1
        self.high = self.n_row.bit_length() - 1

    def send(self, value, move):
        pairs = []
        for i in range(self.n_row):
            for j in range(self.n_col):
                to = move(i, j)
                if to is not None:
                    pairs.append((i * self.n_col + j, to[0] * self.n_col + to[1]))
        return lax.ppermute(value, ("row", "col"), pairs)

    def flip(self, value, bit, holds):
        return self.send(value, lambda i, j: (i ^ (1 << bit), j) if holds(i, j) else None)

    def turn(self, value, by, holds=lambda i, j: True):
        return self.send(value, lambda i, j: (i, (j + by) % self.n_col) if holds(i, j) else None)

    def in_order(self, own, before, after, across):
        parts = []
        for t in range(4):
            away = (t - self.c) % 4
            parts.append(jnp.where(away == 0, own, jnp.where(away == 3, before,
                         jnp.where(away == 1, after, across))))
        return jnp.concatenate(parts, axis=-2)

    def gather_rows(self, x, count):
        has = lambda i, j: i < count
        if self.n_col != 4:
            full = lax.all_gather(x, "col", axis=1, tiled=True)
            return full, [full], [jnp.int32(0)], self.share(full[0], count)
        before = self.turn(x, 1)
        after = self.turn(x, -1)
        tile = self.in_order(x[0], before[0], after[0], self.turn(x[0], 2, has))
        points = self.share(tile, count)
        across = self.turn(before, 1)
        places = [self.c, (self.c - 1) % 4, (self.c + 1) % 4, (self.c + 2) % 4]
        return self.in_order(x, before, after, across), [x, before, after, across], places, points

    def share(self, data, count):
        bits = count.bit_length() - 1
        for bit in range(self.high - 1, bits - 1, -1):
            got = self.flip(data, bit, lambda i, j: i & ~(count - 1) & ((2 << bit) - 1) == 0)
            data = jnp.where((self.r >> bit) & 1 == 0, data, got)
        data = data[None]
        for bit in range(bits):
            got = self.flip(data, bit, lambda i, j: True)
            first = (self.r >> bit) & 1 == 0
            data = jnp.concatenate([jnp.where(first, data, got), jnp.where(first, got, data)])
        return data

    def spread(self, data):
        mask = self.n_col - 1
        for bit in range(self.low - 1, 0, -1):
            got = self.flip(data, bit, lambda i, j: (i ^ j) & mask == 0)
            data = jnp.where((self.r ^ self.c) & (1 << bit) == 0, data, got)
            mask &= ~(1 << bit)
        parts = [data]
        for bit in range(self.low, self.high):
            parts += [self.flip(p, bit, lambda i, j: (i ^ j) & mask == 0) for p in parts]
        return parts, [self.flip(p, 0, lambda i, j: (i ^ j) & 1 == 0) for p in parts]


def local(features):
    grid = Grid()
    r, c = grid.r, grid.c
    tiles_r, _, thin, width = features.shape
    step_tiles = grid.n_row // grid.n_col
    tiles_c = tiles_r * step_tiles
    tile = thin * grid.n_col

    rows, pieces, places, points = grid.gather_rows(features[:, 0], PANEL // tile)
    points = points.reshape(PANEL, width)
    t, sp, bp = factor(points)
    panel_args = (points, t, sp, bp)
    mine, got = [], []
    for piece in pieces:
        here, there = grid.spread(piece)
        mine += here
        got += there

    tau = lambda i: jnp.where(i < PANEL // tile, i, -1)
    x_rows = rows.reshape(tiles_r * tile, width)
    low, *row_args = panel_rows(x_rows, *panel_args, tau(r).astype(jnp.int32).reshape(1))
    info = jnp.stack(
        [(r - c) % grid.n_col == 0, (r - c) // grid.n_col, tau(c), (r ^ c) & 1, r // grid.n_col]
        + places
    ).astype(jnp.int32)
    out = trailing((x_rows, *row_args), mine, got, panel_args, info, step_tiles)
    return (
        low.reshape(tiles_r, 1, tile, PANEL),
        out.reshape(tiles_r, 1, tile, tiles_c, 1, tile),
    )


def solution(mesh):
    return jax.shard_map(
        local,
        mesh=mesh,
        in_specs=(P(None, "row", "col", None),),
        out_specs=(P(None, "row", None, None), P(None, "row", None, None, "col", None)),
        check_vma=False,
    )
```

```python
import functools

import jax
import jax.numpy as jnp
from jax import lax
from jax.experimental import pallas as pl
from jax.experimental.pallas import tpu as pltpu
from jax.sharding import PartitionSpec as P

F = 512
PANEL = 256
TILE = 128
RIDGE = 1.0
EPS = 1e-6

PV = (-2.265364170074463, -4.70527982711792, 7.536093711853027,
      0.7343835830688477, -1.7677195072174072, 0.3254770040512085)
QV = (1.8269329071044922, 3.1679749488830566, -4.871670722961426,
      0.626383364200592, 0.07849788665771484)
TINY = 1e-30
NT = (((1,), (1,)), ((), ()))
VMEM_LIMIT = 60 * 2**20


def dot_nt(a, b):
    return lax.dot_general(a, b, NT, preferred_element_type=jnp.float32)


def dot_hi(a, b, dims):
    return lax.dot_general(
        a, b, (dims, ((), ())), precision=lax.Precision.HIGHEST,
        preferred_element_type=jnp.float32,
    )


def horner(x, coefs):
    acc = coefs[-1]
    for c in coefs[-2::-1]:
        acc = acc * x + c
    return acc


def two_layers(rho):
    a = jnp.maximum(1.0 - rho, TINY)
    b = jnp.maximum(1.0 + rho, TINY)
    u = a * lax.rsqrt(a)
    v = b * lax.rsqrt(b)
    return horner(v, PV) + u * horner(v, QV)


def norm_rows(x):
    xf = x.astype(jnp.float32)
    return jnp.sum(xf * xf, axis=1, keepdims=True) / F


def norm_lanes(x):
    xf = x.astype(jnp.float32)
    sq = xf * xf
    hi = sq.astype(jnp.bfloat16)
    lo = (sq - hi.astype(jnp.float32)).astype(jnp.bfloat16)
    ones = jnp.ones((8, x.shape[1]), jnp.bfloat16)
    return (dot_nt(ones, hi) + dot_nt(ones, lo)) / F


def eye(n):
    return lax.broadcasted_iota(jnp.int32, (n, n), 0) == lax.broadcasted_iota(
        jnp.int32, (n, n), 1
    )


def eliminate(w_ref, t_ref):
    n = TILE
    sub = lax.broadcasted_iota(jnp.int32, (8, n), 0)
    for p in range(0, n, 8):
        a8 = w_ref[p : p + 8, :n]
        e8 = w_ref[p : p + 8, n:]
        cols = [jnp.broadcast_to(a8[:, p + k : p + k + 1], (8, n)) for k in range(8)]
        root = jnp.ones((8, n), jnp.float32)
        invs, ups = [], []
        for k in range(8):
            piv = cols[k][k : k + 1, :]
            inv = 1.0 / piv
            m = jnp.where(sub > k, cols[k] * inv, 0.0)
            ak, ek = a8[k : k + 1, :], e8[k : k + 1, :]
            up = [cols[j][k : k + 1, :] for j in range(k + 1, 8)]
            for j in range(k + 1, 8):
                cols[j] = cols[j] - m * up[j - k - 1]
            a8 = a8 - m * ak
            e8 = e8 - m * ek
            root = jnp.where(sub == k, lax.rsqrt(piv), root)
            invs.append(inv)
            ups.append((ak, ek, up))
        t_ref[p : p + 8, :] = e8 * root
        for g in range(p + 8, n, 8):
            a = w_ref[g : g + 8, :n]
            e = w_ref[g : g + 8, n:]
            cs = [jnp.broadcast_to(a[:, p + k : p + k + 1], (8, n)) for k in range(8)]
            for k in range(8):
                ak, ek, up = ups[k]
                m = cs[k] * invs[k]
                for j in range(k + 1, 8):
                    cs[j] = cs[j] - m * up[j - k - 1]
                a = a - m * ak
                e = e - m * ek
            w_ref[g : g + 8, :n] = a
            w_ref[g : g + 8, n:] = e


def factor_kernel(x_ref, t_ref, sp_ref, bp_ref, k_ref, w_ref, t1_ref, t2_ref):
    x = x_ref[...]
    gq_l = norm_lanes(x)
    s_l = jnp.sqrt(gq_l + EPS)
    b_l = 1.0 / s_l
    sp_ref[...] = s_l
    bp_ref[...] = b_l
    gq = norm_rows(x)
    s = jnp.sqrt(gq + EPS)
    rho = dot_nt(x, x) * ((1.0 / F) / s) * b_l[0:1, :]
    k = two_layers(rho) * (s * s_l[0:1, :])
    k_ref[...] = jnp.where(eye(PANEL), 3.0 * gq + (2.0 * EPS + RIDGE), k)
    h = PANEL // 2
    ident = jnp.where(eye(h), 1.0, 0.0)
    w_ref[:, :h] = k_ref[:h, :h]
    w_ref[:, h:] = ident
    eliminate(w_ref, t1_ref)
    t1 = t1_ref[...]
    l21 = dot_hi(k_ref[h:, :h], t1, ((1,), (1,)))
    w_ref[:, :h] = k_ref[h:, h:] - dot_hi(l21, l21, ((1,), (1,)))
    w_ref[:, h:] = ident
    eliminate(w_ref, t2_ref)
    t2 = t2_ref[...]
    t_ref[:h, :h] = t1
    t_ref[:h, h:] = jnp.zeros((h, h), jnp.float32)
    t_ref[h:, :h] = -dot_hi(t2, dot_hi(l21, t1, ((1,), (0,))), ((1,), (0,)))
    t_ref[h:, h:] = t2


def factor(points):
    full = jax.ShapeDtypeStruct((PANEL, PANEL), jnp.float32)
    vec = jax.ShapeDtypeStruct((8, PANEL), jnp.float32)
    return pl.pallas_call(
        factor_kernel,
        out_shape=[full, vec, vec],
        scratch_shapes=[
            pltpu.VMEM((PANEL, PANEL), jnp.float32),
            pltpu.VMEM((TILE, 2 * TILE), jnp.float32),
            pltpu.VMEM((TILE, TILE), jnp.float32),
            pltpu.VMEM((TILE, TILE), jnp.float32),
        ],
        compiler_params=pltpu.CompilerParams(vmem_limit_bytes=VMEM_LIMIT),
        cost_estimate=pl.CostEstimate(flops=12 * 10**9, bytes_accessed=10**6, transcendentals=0),
        name="factor",
    )(points)


def panel_block(x, pts, sp, bp, k_ref):
    gq = norm_rows(x)
    s = jnp.sqrt(gq + EPS)
    a = (1.0 / F) / s
    k_ref[...] = dot_nt(x, pts)
    for g in range(0, x.shape[0], 16):
        rows = slice(g, g + 16)
        rho = k_ref[rows, :] * a[rows, :] * bp
        k_ref[rows, :] = two_layers(rho) * (s[rows, :] * sp)
    return s, a, 3.0 * gq + (2.0 * EPS + RIDGE)


def set_diagonal(k_ref, diag, hit):
    for half in range(PANEL // TILE):

        @pl.when(hit == half)
        def _():
            cols = slice(half * TILE, (half + 1) * TILE)
            k_ref[:TILE, cols] = jnp.where(eye(TILE), diag[:TILE, :], k_ref[:TILE, cols])


def split(low):
    hi = low.astype(jnp.bfloat16)
    return hi, (low - hi.astype(jnp.float32)).astype(jnp.bfloat16)


def panel_kernel(tau_ref, x_ref, pts_ref, t_ref, sp_ref, bp_ref,
                 l_ref, cat_ref, s_ref, a_ref, d_ref, k_ref):
    s, a, diag = panel_block(x_ref[...], pts_ref[...], sp_ref[0:1, :], bp_ref[0:1, :], k_ref)
    set_diagonal(k_ref, diag, jnp.where(pl.program_id(0) == 0, tau_ref[0], -1))
    low = dot_hi(k_ref[...], t_ref[...], ((1,), (1,)))
    hi, lo = split(low)
    l_ref[...] = low
    cat_ref[:, :PANEL] = hi
    cat_ref[:, PANEL : 2 * PANEL] = hi
    cat_ref[:, 2 * PANEL :] = lo
    s_ref[...] = jnp.broadcast_to(s, s_ref.shape)
    a_ref[...] = jnp.broadcast_to(a, a_ref.shape)
    left = diag - jnp.sum(low * low, axis=1, keepdims=True)
    d_ref[...] = jnp.broadcast_to(left, d_ref.shape)


def pick(total, options):
    for o in options:
        if total % o == 0:
            return o
    return total


def panel_rows(x, points, t, sp, bp, tau):
    m = x.shape[0]
    block = pick(m, (512, 384, 256, 128))
    const = lambda shape: pl.BlockSpec(shape, lambda i: (0, 0))
    by_row = lambda width: pl.BlockSpec((block, width), lambda i: (i, 0))
    f32 = lambda *shape: jax.ShapeDtypeStruct(shape, jnp.float32)
    return pl.pallas_call(
        panel_kernel,
        grid=(m // block,),
        in_specs=[
            pl.BlockSpec(memory_space=pltpu.SMEM),
            by_row(F), const((PANEL, F)), const((PANEL, PANEL)),
            const((8, PANEL)), const((8, PANEL)),
        ],
        out_specs=[by_row(PANEL), by_row(3 * PANEL)] + [by_row(128)] * 3,
        out_shape=[f32(m, PANEL), jax.ShapeDtypeStruct((m, 3 * PANEL), jnp.bfloat16),
                   f32(m, 128), f32(m, 128), f32(m, 128)],
        scratch_shapes=[pltpu.VMEM((block, PANEL), jnp.float32)],
        compiler_params=pltpu.CompilerParams(vmem_limit_bytes=VMEM_LIMIT),
        cost_estimate=pl.CostEstimate(
            flops=12 * m * PANEL * (F + 6 * PANEL), bytes_accessed=m * 4096, transcendentals=0
        ),
        name="panel_rows",
    )(tau, x, points, t, sp, bp)


def trailing_kernel(rb, tb, blocks, steps, step_tiles, fold, arrays, info, *refs):
    mine, got, refs = refs[:arrays], refs[arrays : 2 * arrays], refs[2 * arrays :]
    pts, t_ref, sp_ref, bp_ref, xr, xr_next, lr, lr_next, sr, ar, dr = refs[:11]
    out, xc, lc, sc, bc, k_ref, ga, ma, gb, mb, sem = refs[-11:]
    if fold:
        out = out.reshape(rb * tb, TILE)
    q = pl.program_id(0)
    i, j = q // blocks, q % blocks
    cb = tb * TILE // 2
    per = cb // TILE

    def load(arrays):
        moves, base = [], 0
        for k in range(0, len(arrays), step_tiles):
            for entry, src in enumerate(arrays[k : k + step_tiles]):
                for tile in range(src.shape[0]):
                    at = ((base + tile) * step_tiles + (info[4] ^ entry)) * TILE
                    to = xc.at[pl.ds(pl.multiple_of(at, TILE), TILE)]
                    moves.append(pltpu.make_async_copy(src.at[tile], to, sem))
            base += arrays[k].shape[0]
        for move in moves:
            move.start()
        for move in moves:
            move.wait()

    def columns(b):
        size = k_ref.shape[0]
        rows = pl.ds(pl.multiple_of(b * size, size), size)
        s, _, diag = panel_block(xc[rows, :], pts[...], sp_ref[0:1, :], bp_ref[0:1, :], k_ref)
        set_diagonal(k_ref, diag, jnp.where(b == 0, info[2], -1))
        hi, lo = split(dot_hi(k_ref[...], t_ref[...], ((1,), (1,))))
        lc[rows, :PANEL] = hi
        lc[rows, PANEL : 2 * PANEL] = lo
        lc[rows, 2 * PANEL :] = hi
        for g in range(0, size, TILE):
            wide = jnp.broadcast_to(s[g : g + TILE, :], (TILE, TILE)).T[0:8, :]
            lanes = pl.ds(pl.multiple_of(b * size + g, TILE), TILE)
            sc[:, lanes] = wide
            bc[:, lanes] = 1.0 / wide

    def multiply(x, l, col, g, m):
        cols = pl.ds(pl.multiple_of(col, cb), cb)
        g[...] = dot_nt(x[...], xc[cols, :])
        m[...] = dot_nt(l[...], lc[cols, :])

    def finish(half, g, m):
        for tile in range(per):
            lanes = pl.ds(pl.multiple_of(j * (tb * TILE) + half * cb + tile * TILE, TILE), TILE)
            s_col = sc[0:1, lanes]
            b_col = bc[0:1, lanes]
            here = slice(tile * TILE, (tile + 1) * TILE)
            for k in range(0, rb, 16):
                rows = slice(k, k + 16)
                rho = g[rows, here] * ar[rows, :] * b_col
                val = two_layers(rho) * (sr[rows, :] * s_col) - m[rows, here]
                out[pl.ds(k * tb + half * per + tile, 16, stride=tb), :] = val

    @pl.when(q == 0)
    def _():
        @pl.when(info[3] == 0)
        def _():
            load(mine)

        @pl.when(info[3] != 0)
        def _():
            load(got)

        @pl.loop(0, xc.shape[0] // k_ref.shape[0])
        def _(b):
            columns(b)

        multiply(xr, lr, 0, ga, ma)

    multiply(xr, lr, j * (tb * TILE) + cb, gb, mb)
    finish(0, ga, ma)
    after = jnp.minimum(q + 1, steps - 1) % blocks
    multiply(xr_next, lr_next, after * (tb * TILE), ga, ma)
    finish(1, gb, mb)

    for tile in range(rb // TILE):
        col = (i * (rb // TILE) + tile) * step_tiles + info[1] - j * tb

        @pl.when((info[0] == 1) & (col >= 0) & (col < tb))
        def _():
            for k in range(0, TILE, 16):
                rows = slice(tile * TILE + k, tile * TILE + k + 16)
                same = lax.broadcasted_iota(jnp.int32, (16, TILE), 1) == (
                    lax.broadcasted_iota(jnp.int32, (16, TILE), 0) + k
                )
                at = pl.ds((tile * TILE + k) * tb + col, 16, stride=tb)
                out[at, :] = jnp.where(same, dr[rows, :], out[at, :])


def trailing(row_args, mine, got, panel_args, info, step_tiles):
    x_rows, cat_rows, s, a, d = row_args
    m = x_rows.shape[0]
    tiles_c = m // TILE * step_tiles
    n = tiles_c * TILE
    fold = tiles_c % 8 == 0
    tb = 8 if fold else tiles_c
    rb = pick(m, (512, 384, 256, 128))
    cb = tb * TILE // 2
    blocks = n // (tb * TILE)
    steps = m // rb * blocks
    const = lambda shape: pl.BlockSpec(shape, lambda q: (0, 0))
    cur = lambda width: pl.BlockSpec((rb, width), lambda q: (q // blocks, 0))
    nxt = lambda width: pl.BlockSpec(
        (rb, width), lambda q: (jnp.minimum(q + 1, steps - 1) // blocks, 0)
    )
    hbm = pl.BlockSpec(memory_space=pl.ANY)
    if fold:
        shape = (m, tiles_c, TILE)
        spec = pl.BlockSpec((rb, tb, TILE), lambda q: (q // blocks, q % blocks, 0))
    else:
        shape = (m * tb, TILE)
        spec = pl.BlockSpec((rb * tb, TILE), lambda q: (q, 0))
    square = pltpu.VMEM((rb, cb), jnp.float32)
    return pl.pallas_call(
        functools.partial(
            trailing_kernel, rb, tb, blocks, steps, step_tiles, fold, len(mine)
        ),
        grid=(steps,),
        in_specs=[pl.BlockSpec(memory_space=pltpu.SMEM)] + [hbm] * (2 * len(mine)) + [
            const((PANEL, F)), const((PANEL, PANEL)), const((8, PANEL)), const((8, PANEL)),
            cur(F), nxt(F), cur(3 * PANEL), nxt(3 * PANEL), cur(128), cur(128), cur(128),
        ],
        out_specs=spec,
        out_shape=jax.ShapeDtypeStruct(shape, jnp.float32),
        scratch_shapes=[
            pltpu.VMEM((n, F), jnp.bfloat16),
            pltpu.VMEM((n, 3 * PANEL), jnp.bfloat16),
            pltpu.VMEM((8, n), jnp.float32),
            pltpu.VMEM((8, n), jnp.float32),
            pltpu.VMEM((pick(n, (512, 384, 256, 128)), PANEL), jnp.float32),
            square, square, square, square,
            pltpu.SemaphoreType.DMA,
        ],
        compiler_params=pltpu.CompilerParams(vmem_limit_bytes=VMEM_LIMIT),
        cost_estimate=pl.CostEstimate(
            flops=8 * m * n * (F + 3 * PANEL), bytes_accessed=m * n * 4, transcendentals=0
        ),
        name="trailing",
    )(info, *mine, *got, *panel_args, x_rows, x_rows, cat_rows, cat_rows, s, a, d)


class Grid:
    def __init__(self):
        self.n_row, self.n_col = lax.axis_size("row"), lax.axis_size("col")
        self.r, self.c = lax.axis_index("row"), lax.axis_index("col")
        self.low = self.n_col.bit_length() - 1
        self.high = self.n_row.bit_length() - 1

    def send(self, value, move):
        pairs = []
        for i in range(self.n_row):
            for j in range(self.n_col):
                to = move(i, j)
                if to is not None:
                    pairs.append((i * self.n_col + j, to[0] * self.n_col + to[1]))
        return lax.ppermute(value, ("row", "col"), pairs)

    def flip(self, value, bit, holds):
        return self.send(value, lambda i, j: (i ^ (1 << bit), j) if holds(i, j) else None)

    def turn(self, value, by, holds=lambda i, j: True):
        return self.send(value, lambda i, j: (i, (j + by) % self.n_col) if holds(i, j) else None)

    def in_order(self, own, before, after, across):
        parts = []
        for t in range(4):
            away = (t - self.c) % 4
            parts.append(jnp.where(away == 0, own, jnp.where(away == 3, before,
                         jnp.where(away == 1, after, across))))
        return jnp.concatenate(parts, axis=-2)

    def gather_rows(self, x, count):
        has = lambda i, j: i < count
        if self.n_col != 4:
            full = lax.all_gather(x, "col", axis=1, tiled=True)
            return full, self.share(full[0], count, None)
        before = self.turn(x, 1)
        after = self.turn(x, -1)
        across = self.turn(before, 1)
        tile = self.in_order(x[0], before[0], after[0], self.turn(before[0], 1, has))
        points = self.share(tile, count, across)
        return self.in_order(x, before, after, across), points

    def share(self, data, count, gate):
        bits = count.bit_length() - 1
        for bit in range(bits, self.high):
            got = self.flip(data, bit, lambda i, j: i >> bit == 0)
            data = jnp.where(self.r >> bit == 0, data, got)
            if bit == bits:
                data = tie(data, gate)
        data = data[None]
        for bit in range(bits):
            got = self.flip(data, bit, lambda i, j: True)
            first = (self.r >> bit) & 1 == 0
            data = jnp.concatenate([jnp.where(first, data, got), jnp.where(first, got, data)])
        return data

    def spread(self, data, high_first, second, last):
        mask = [self.n_col - 1]

        def copies(parts):
            for bit in range(self.low - 1, 0, -1):
                holds = lambda i, j: (i ^ j) & mask[0] == 0
                own = (self.r ^ self.c) & (1 << bit) == 0
                parts = [jnp.where(own, p, self.flip(p, bit, holds)) for p in parts]
                mask[0] &= ~(1 << bit)
            return parts

        def swaps(parts):
            for bit in range(self.low, self.high):
                holds = lambda i, j: (i ^ j) & mask[0] == 0
                parts = parts + [self.flip(p, bit, holds) for p in parts]
            return parts

        steps = (swaps, copies) if high_first else (copies, swaps)
        parts = steps[0]([data])
        parts = steps[1]([tie(p, second) for p in parts])
        parts = [tie(p, last) for p in parts]
        return parts, [self.flip(p, 0, lambda i, j: (i ^ j) & 1 == 0) for p in parts]


def tie(value, earlier):
    return value if earlier is None else lax.optimization_barrier((value, earlier))[0]


def local(features):
    grid = Grid()
    r, c = grid.r, grid.c
    tiles_r, _, thin, width = features.shape
    step_tiles = grid.n_row // grid.n_col
    tiles_c = tiles_r * step_tiles
    tile = thin * grid.n_col

    rows, points = grid.gather_rows(features[:, 0], PANEL // tile)
    x_rows = rows.reshape(tiles_r * tile, width)
    points = points.reshape(PANEL, width)
    t, sp, bp = factor(points)
    panel_args = (points, t, sp, bp)
    tau = lambda i: jnp.where(i < PANEL // tile, i, -1)
    low, *row_args = panel_rows(x_rows, *panel_args, tau(r).astype(jnp.int32).reshape(1))

    cut = tiles_r * 2 // 3 if tiles_r % 3 == 0 else tiles_r
    pieces = [rows[:cut], rows[cut:]] if cut < tiles_r else [rows]
    mine, got = [], []
    for k, piece in enumerate(pieces):
        here, there = grid.spread(piece, k > 0, t, row_args[0])
        mine += here
        got += there
    info = jnp.stack([
        (r - c) % grid.n_col == 0, (r - c) // grid.n_col, tau(c), (r ^ c) & 1, r // grid.n_col,
    ]).astype(jnp.int32)
    out = trailing((x_rows, *row_args), mine, got, panel_args, info, step_tiles)
    return (
        low.reshape(tiles_r, 1, tile, PANEL),
        out.reshape(tiles_r, 1, tile, tiles_c, 1, tile),
    )


def solution(mesh):
    return jax.shard_map(
        local,
        mesh=mesh,
        in_specs=(P(None, "row", "col", None),),
        out_specs=(P(None, "row", None, None), P(None, "row", None, None, "col", None)),
        check_vma=False,
    )
```

```python
import functools

import jax
import jax.numpy as jnp
from jax import lax
from jax.experimental import pallas as pl
from jax.experimental.pallas import tpu as pltpu
from jax.sharding import PartitionSpec as P

F = 512
PANEL = 256
TILE = 128
RIDGE = 1.0
EPS = 1e-6

PV = (-2.265364170074463, -4.70527982711792, 7.536093711853027,
      0.7343835830688477, -1.7677195072174072, 0.3254770040512085)
QV = (1.8269329071044922, 3.1679749488830566, -4.871670722961426,
      0.626383364200592, 0.07849788665771484)
TINY = 1e-30
NT = (((1,), (1,)), ((), ()))
VMEM_LIMIT = 60 * 2**20


def dot_nt(a, b):
    return lax.dot_general(a, b, NT, preferred_element_type=jnp.float32)


def dot_hi(a, b, dims):
    return lax.dot_general(
        a, b, (dims, ((), ())), precision=lax.Precision.HIGHEST,
        preferred_element_type=jnp.float32,
    )


def horner(x, coefs):
    acc = coefs[-1]
    for c in coefs[-2::-1]:
        acc = acc * x + c
    return acc


def two_layers(rho):
    a = jnp.maximum(1.0 - rho, TINY)
    b = jnp.maximum(1.0 + rho, TINY)
    u = a * lax.rsqrt(a)
    v = b * lax.rsqrt(b)
    return horner(v, PV) + u * horner(v, QV)


def norm_rows(x):
    xf = x.astype(jnp.float32)
    return jnp.sum(xf * xf, axis=1, keepdims=True) / F


def norm_lanes(x):
    xf = x.astype(jnp.float32)
    sq = xf * xf
    hi = sq.astype(jnp.bfloat16)
    lo = (sq - hi.astype(jnp.float32)).astype(jnp.bfloat16)
    ones = jnp.ones((8, x.shape[1]), jnp.bfloat16)
    return (dot_nt(ones, hi) + dot_nt(ones, lo)) / F


def eye(n):
    return lax.broadcasted_iota(jnp.int32, (n, n), 0) == lax.broadcasted_iota(
        jnp.int32, (n, n), 1
    )


def eliminate(w_ref, t_ref):
    n = TILE
    sub = lax.broadcasted_iota(jnp.int32, (8, n), 0)
    for p in range(0, n, 8):
        a8 = w_ref[p : p + 8, :n]
        e8 = w_ref[p : p + 8, n:]
        cols = [jnp.broadcast_to(a8[:, p + k : p + k + 1], (8, n)) for k in range(8)]
        root = jnp.ones((8, n), jnp.float32)
        invs, ups = [], []
        for k in range(8):
            piv = cols[k][k : k + 1, :]
            inv = 1.0 / piv
            m = jnp.where(sub > k, cols[k], 0.0) * inv
            ak, ek = a8[k : k + 1, :], e8[k : k + 1, :]
            up = [cols[j][k : k + 1, :] for j in range(k + 1, 8)]
            for j in range(k + 1, 8):
                cols[j] = cols[j] - m * up[j - k - 1]
            a8 = a8 - m * ak
            e8 = e8 - m * ek
            root = jnp.where(sub == k, lax.rsqrt(piv), root)
            invs.append(inv)
            ups.append((ak, ek, up))
        t_ref[p : p + 8, :] = e8 * root
        for g in range(p + 8, n, 8):
            a = w_ref[g : g + 8, :n]
            e = w_ref[g : g + 8, n:]
            cs = [jnp.broadcast_to(a[:, p + k : p + k + 1], (8, n)) for k in range(8)]
            for k in range(8):
                ak, ek, up = ups[k]
                m = cs[k] * invs[k]
                for j in range(k + 1, 8):
                    cs[j] = cs[j] - m * up[j - k - 1]
                a = a - m * ak
                e = e - m * ek
            w_ref[g : g + 8, :n] = a
            w_ref[g : g + 8, n:] = e


def factor_kernel(x_ref, t_ref, sp_ref, bp_ref, k_ref, w_ref, t1_ref, t2_ref):
    x = x_ref[...]
    gq_l = norm_lanes(x)
    b_l = lax.rsqrt(gq_l + EPS)
    s_l = (gq_l + EPS) * b_l
    sp_ref[...] = s_l
    bp_ref[...] = b_l
    gq = norm_rows(x)
    s = jnp.sqrt(gq + EPS)
    rho = dot_nt(x, x) * ((1.0 / F) / s) * b_l[0:1, :]
    k = two_layers(rho) * (s * s_l[0:1, :])
    k_ref[...] = jnp.where(eye(PANEL), 3.0 * gq + (2.0 * EPS + RIDGE), k)
    h = PANEL // 2
    ident = jnp.where(eye(h), 1.0, 0.0)
    w_ref[:, :h] = k_ref[:h, :h]
    w_ref[:, h:] = ident
    eliminate(w_ref, t1_ref)
    t1 = t1_ref[...]
    l21 = dot_hi(k_ref[h:, :h], t1, ((1,), (1,)))
    w_ref[:, :h] = k_ref[h:, h:] - dot_hi(l21, l21, ((1,), (1,)))
    w_ref[:, h:] = ident
    eliminate(w_ref, t2_ref)
    t2 = t2_ref[...]
    t_ref[:h, :h] = t1
    t_ref[:h, h:] = jnp.zeros((h, h), jnp.float32)
    t_ref[h:, :h] = -dot_hi(t2, dot_hi(l21, t1, ((1,), (0,))), ((1,), (0,)))
    t_ref[h:, h:] = t2


def factor(points):
    full = jax.ShapeDtypeStruct((PANEL, PANEL), jnp.float32)
    vec = jax.ShapeDtypeStruct((8, PANEL), jnp.float32)
    return pl.pallas_call(
        factor_kernel,
        out_shape=[full, vec, vec],
        scratch_shapes=[
            pltpu.VMEM((PANEL, PANEL), jnp.float32),
            pltpu.VMEM((TILE, 2 * TILE), jnp.float32),
            pltpu.VMEM((TILE, TILE), jnp.float32),
            pltpu.VMEM((TILE, TILE), jnp.float32),
        ],
        compiler_params=pltpu.CompilerParams(vmem_limit_bytes=VMEM_LIMIT),
        cost_estimate=pl.CostEstimate(flops=12 * 10**9, bytes_accessed=10**6, transcendentals=0),
        name="factor",
    )(points)


def panel_block(x_ref, pts, sp, bp, k_ref):
    m = x_ref.shape[0]
    part = m // 2 if m % 32 == 0 else m
    norms = []
    for h in range(0, m, part):
        x = x_ref[h : h + part, :]
        gq = norm_rows(x)
        q = gq + EPS
        inv = lax.rsqrt(q)
        s = q * inv
        a = inv * (1.0 / F)
        k_ref[h : h + part, :] = dot_nt(x, pts)
        for g in range(0, part, 16):
            rows = slice(h + g, h + g + 16)
            rho = k_ref[rows, :] * a[g : g + 16, :] * bp
            k_ref[rows, :] = two_layers(rho) * (s[g : g + 16, :] * sp)
        norms.append((h, part, s, a, 3.0 * gq + (2.0 * EPS + RIDGE)))
    return norms


def set_diagonal(k_ref, diag, hit):
    for half in range(PANEL // TILE):
        cols = slice(half * TILE, (half + 1) * TILE)
        here = eye(TILE) & (hit == half)
        k_ref[:TILE, cols] = jnp.where(here, diag[:TILE, :], k_ref[:TILE, cols])


def split(low):
    hi = low.astype(jnp.bfloat16)
    return hi, (low - hi.astype(jnp.float32)).astype(jnp.bfloat16)


def panel_kernel(tau_ref, x_ref, pts_ref, t_ref, sp_ref, bp_ref,
                 l_ref, cat_ref, s_ref, a_ref, d_ref, k_ref):
    norms = panel_block(x_ref, pts_ref[...], sp_ref[0:1, :], bp_ref[0:1, :], k_ref)
    set_diagonal(k_ref, norms[0][4], jnp.where(pl.program_id(0) == 0, tau_ref[0], -1))
    for h, part, s, a, diag in norms:
        rows = slice(h, h + part)
        low = dot_hi(k_ref[rows, :], t_ref[...], ((1,), (1,)))
        hi, lo = split(low)
        l_ref[rows, :] = low
        cat_ref[rows, :PANEL] = hi
        cat_ref[rows, PANEL : 2 * PANEL] = hi
        cat_ref[rows, 2 * PANEL :] = lo
        s_ref[rows, :] = jnp.broadcast_to(s, (part, 128))
        a_ref[rows, :] = jnp.broadcast_to(a, (part, 128))
        left = diag - jnp.sum(low * low, axis=1, keepdims=True)
        d_ref[rows, :] = jnp.broadcast_to(left, (part, 128))


def pick(total, options):
    for o in options:
        if total % o == 0:
            return o
    return total


def panel_rows(x, points, t, sp, bp, tau):
    m = x.shape[0]
    block = pick(m, (512, 384, 256, 128))
    const = lambda shape: pl.BlockSpec(shape, lambda i: (0, 0))
    by_row = lambda width: pl.BlockSpec((block, width), lambda i: (i, 0))
    f32 = lambda *shape: jax.ShapeDtypeStruct(shape, jnp.float32)
    return pl.pallas_call(
        panel_kernel,
        grid=(m // block,),
        in_specs=[
            pl.BlockSpec(memory_space=pltpu.SMEM),
            by_row(F), const((PANEL, F)), const((PANEL, PANEL)),
            const((8, PANEL)), const((8, PANEL)),
        ],
        out_specs=[by_row(PANEL), by_row(3 * PANEL)] + [by_row(128)] * 3,
        out_shape=[f32(m, PANEL), jax.ShapeDtypeStruct((m, 3 * PANEL), jnp.bfloat16),
                   f32(m, 128), f32(m, 128), f32(m, 128)],
        scratch_shapes=[pltpu.VMEM((block, PANEL), jnp.float32)],
        compiler_params=pltpu.CompilerParams(vmem_limit_bytes=VMEM_LIMIT),
        cost_estimate=pl.CostEstimate(
            flops=12 * m * PANEL * (F + 6 * PANEL), bytes_accessed=m * 4096, transcendentals=0
        ),
        name="panel_rows",
    )(tau, x, points, t, sp, bp)


def trailing_kernel(rb, tb, blocks, steps, step_tiles, fold, arrays, info, *refs):
    mine, got, refs = refs[:arrays], refs[arrays : 2 * arrays], refs[2 * arrays :]
    pts, t_ref, sp_ref, bp_ref, xr, xr_next, lr, lr_next, sr, ar, dr = refs[:11]
    out, xc, lc, sc, bc, k_ref, ga, ma, gb, mb, sem = refs[-11:]
    if fold:
        out = out.reshape(rb * tb, TILE)
    q = pl.program_id(0)
    i, j = q // blocks, q % blocks
    cb = tb * TILE // 2
    per = cb // TILE

    size = k_ref.shape[0]

    def load(arrays):
        base = 0
        for k in range(0, len(arrays), step_tiles):
            for tile in range(arrays[k].shape[0]):
                for entry, src in enumerate(arrays[k : k + step_tiles]):
                    at = ((base + tile) * step_tiles + (info[4] ^ entry)) * TILE
                    to = xc.at[pl.ds(pl.multiple_of(at, TILE), TILE)]
                    pltpu.make_async_copy(src.at[tile], to, sem.at[at // size]).start()
            base += arrays[k].shape[0]

    def columns(b):
        rows = pl.ds(pl.multiple_of(b * size, size), size)
        pltpu.make_async_copy(xc.at[rows], xc.at[rows], sem.at[b]).wait()
        norms = panel_block(xc.at[rows], pts[...], sp_ref[0:1, :], bp_ref[0:1, :], k_ref)
        set_diagonal(k_ref, norms[0][4], jnp.where(b == 0, info[2], -1))
        for h, part, s, _, _ in norms:
            hi, lo = split(dot_hi(k_ref[h : h + part, :], t_ref[...], ((1,), (1,))))
            to = pl.ds(pl.multiple_of(b * size + h, part), part)
            lc[to, :PANEL] = hi
            lc[to, PANEL : 2 * PANEL] = lo
            lc[to, 2 * PANEL :] = hi
            for g in range(0, part, TILE):
                wide = jnp.broadcast_to(s[g : g + TILE, :], (TILE, TILE)).T[0:8, :]
                lanes = pl.ds(pl.multiple_of(b * size + h + g, TILE), TILE)
                sc[:, lanes] = wide
                bc[:, lanes] = 1.0 / wide

    def multiply(x, l, col, g, m):
        cols = pl.ds(pl.multiple_of(col, cb), cb)
        g[...] = dot_nt(x[...], xc[cols, :])
        m[...] = dot_nt(l[...], lc[cols, :])

    def finish(half, g, m):
        for tile in range(per):
            lanes = pl.ds(pl.multiple_of(j * (tb * TILE) + half * cb + tile * TILE, TILE), TILE)
            s_col = sc[0:1, lanes]
            b_col = bc[0:1, lanes]
            here = slice(tile * TILE, (tile + 1) * TILE)
            for k in range(0, rb, 16):
                rows = slice(k, k + 16)
                rho = g[rows, here] * ar[rows, :] * b_col
                val = two_layers(rho) * (sr[rows, :] * s_col) - m[rows, here]
                out[pl.ds(k * tb + half * per + tile, 16, stride=tb), :] = val

    @pl.when(q == 0)
    def _():
        @pl.when(info[3] == 0)
        def _():
            load(mine)

        @pl.when(info[3] != 0)
        def _():
            load(got)

        @pl.loop(0, xc.shape[0] // size)
        def _(b):
            columns(b)

        multiply(xr, lr, 0, ga, ma)

    multiply(xr, lr, j * (tb * TILE) + cb, gb, mb)
    finish(0, ga, ma)
    after = jnp.minimum(q + 1, steps - 1) % blocks
    multiply(xr_next, lr_next, after * (tb * TILE), ga, ma)
    finish(1, gb, mb)

    for tile in range(rb // TILE):
        col = (i * (rb // TILE) + tile) * step_tiles + info[1] - j * tb

        @pl.when((info[0] == 1) & (col >= 0) & (col < tb))
        def _():
            for k in range(0, TILE, 16):
                rows = slice(tile * TILE + k, tile * TILE + k + 16)
                same = lax.broadcasted_iota(jnp.int32, (16, TILE), 1) == (
                    lax.broadcasted_iota(jnp.int32, (16, TILE), 0) + k
                )
                at = pl.ds((tile * TILE + k) * tb + col, 16, stride=tb)
                out[at, :] = jnp.where(same, dr[rows, :], out[at, :])


def trailing(row_args, mine, got, panel_args, info, step_tiles):
    x_rows, cat_rows, s, a, d = row_args
    m = x_rows.shape[0]
    tiles_c = m // TILE * step_tiles
    n = tiles_c * TILE
    fold = tiles_c % 8 == 0
    tb = 8 if fold else tiles_c
    rb = pick(m, (512, 384, 256, 128))
    cb = tb * TILE // 2
    blocks = n // (tb * TILE)
    steps = m // rb * blocks
    size = pick(n, (512, 256))
    const = lambda shape: pl.BlockSpec(shape, lambda q: (0, 0))
    cur = lambda width: pl.BlockSpec((rb, width), lambda q: (q // blocks, 0))
    nxt = lambda width: pl.BlockSpec(
        (rb, width), lambda q: (jnp.minimum(q + 1, steps - 1) // blocks, 0)
    )
    hbm = pl.BlockSpec(memory_space=pl.ANY)
    if fold:
        shape = (m, tiles_c, TILE)
        spec = pl.BlockSpec((rb, tb, TILE), lambda q: (q // blocks, q % blocks, 0))
    else:
        shape = (m * tb, TILE)
        spec = pl.BlockSpec((rb * tb, TILE), lambda q: (q, 0))
    square = pltpu.VMEM((rb, cb), jnp.float32)
    return pl.pallas_call(
        functools.partial(
            trailing_kernel, rb, tb, blocks, steps, step_tiles, fold, len(mine)
        ),
        grid=(steps,),
        in_specs=[pl.BlockSpec(memory_space=pltpu.SMEM)] + [hbm] * (2 * len(mine)) + [
            const((PANEL, F)), const((PANEL, PANEL)), const((8, PANEL)), const((8, PANEL)),
            cur(F), nxt(F), cur(3 * PANEL), nxt(3 * PANEL), cur(128), cur(128), cur(128),
        ],
        out_specs=spec,
        out_shape=jax.ShapeDtypeStruct(shape, jnp.float32),
        scratch_shapes=[
            pltpu.VMEM((n, F), jnp.bfloat16),
            pltpu.VMEM((n, 3 * PANEL), jnp.bfloat16),
            pltpu.VMEM((8, n), jnp.float32),
            pltpu.VMEM((8, n), jnp.float32),
            pltpu.VMEM((size, PANEL), jnp.float32),
            square, square, square, square,
            pltpu.SemaphoreType.DMA((n // size,)),
        ],
        compiler_params=pltpu.CompilerParams(vmem_limit_bytes=VMEM_LIMIT),
        cost_estimate=pl.CostEstimate(
            flops=8 * m * n * (F + 3 * PANEL), bytes_accessed=m * n * 4, transcendentals=0
        ),
        name="trailing",
    )(info, *mine, *got, *panel_args, x_rows, x_rows, cat_rows, cat_rows, s, a, d)


class Grid:
    def __init__(self):
        self.n_row, self.n_col = lax.axis_size("row"), lax.axis_size("col")
        self.r, self.c = lax.axis_index("row"), lax.axis_index("col")
        self.low = self.n_col.bit_length() - 1
        self.high = self.n_row.bit_length() - 1

    def send(self, value, move):
        pairs = []
        for i in range(self.n_row):
            for j in range(self.n_col):
                to = move(i, j)
                if to is not None:
                    pairs.append((i * self.n_col + j, to[0] * self.n_col + to[1]))
        return lax.ppermute(value, ("row", "col"), pairs)

    def flip(self, value, bit, holds):
        return self.send(value, lambda i, j: (i ^ (1 << bit), j) if holds(i, j) else None)

    def turn(self, value, by, holds=lambda i, j: True):
        return self.send(value, lambda i, j: (i, (j + by) % self.n_col) if holds(i, j) else None)

    def in_order(self, own, before, after, across):
        parts = []
        for t in range(4):
            away = (t - self.c) % 4
            parts.append(jnp.where(away == 0, own, jnp.where(away == 3, before,
                         jnp.where(away == 1, after, across))))
        return jnp.concatenate(parts, axis=-2)

    def gather_rows(self, x, count):
        has = lambda i, j: i < count
        if self.n_col != 4:
            full = lax.all_gather(x, "col", axis=1, tiled=True)
            return full, self.share(full[0], count, None)
        before = self.turn(x, 1)
        after = self.turn(x, -1)
        across = self.turn(before, 1)
        tile = self.in_order(x[0], before[0], after[0], self.turn(before[0], 1, has))
        points = self.share(tile, count, across)
        return self.in_order(x, before, after, across), points

    def share(self, data, count, gate):
        bits = count.bit_length() - 1
        for bit in range(bits, self.high):
            got = self.flip(data, bit, lambda i, j: i >> bit == 0)
            data = jnp.where(self.r >> bit == 0, data, got)
            if bit == bits:
                data = tie(data, gate)
        data = data[None]
        for bit in range(bits):
            got = self.flip(data, bit, lambda i, j: True)
            first = (self.r >> bit) & 1 == 0
            data = jnp.concatenate([jnp.where(first, data, got), jnp.where(first, got, data)])
        return data

    def spread(self, data, high_first, second, last):
        mask = [self.n_col - 1]

        def copies(parts):
            for bit in range(self.low - 1, 0, -1):
                holds = lambda i, j: (i ^ j) & mask[0] == 0
                own = (self.r ^ self.c) & (1 << bit) == 0
                data = parts[0] if len(parts) == 1 else jnp.stack(parts)
                data = jnp.where(own, data, self.flip(data, bit, holds))
                parts = [data] if len(parts) == 1 else list(data)
                mask[0] &= ~(1 << bit)
            return parts

        def swaps(parts):
            for bit in range(self.low, self.high):
                holds = lambda i, j: (i ^ j) & mask[0] == 0
                parts = parts + [self.flip(p, bit, holds) for p in parts]
            return parts

        steps = (swaps, copies) if high_first else (copies, swaps)
        parts = steps[0]([data])
        parts = steps[1]([tie(p, second) for p in parts])
        parts = [tie(p, last) for p in parts]
        return parts, [self.flip(p, 0, lambda i, j: (i ^ j) & 1 == 0) for p in parts]


def tie(value, earlier):
    return value if earlier is None else lax.optimization_barrier((value, earlier))[0]


def local(features):
    grid = Grid()
    r, c = grid.r, grid.c
    tiles_r, _, thin, width = features.shape
    step_tiles = grid.n_row // grid.n_col
    tiles_c = tiles_r * step_tiles
    tile = thin * grid.n_col

    rows, points = grid.gather_rows(features[:, 0], PANEL // tile)
    x_rows = rows.reshape(tiles_r * tile, width)
    points = points.reshape(PANEL, width)
    t, sp, bp = factor(points)
    panel_args = (points, t, sp, bp)
    tau = lambda i: jnp.where(i < PANEL // tile, i, -1)
    low, *row_args = panel_rows(x_rows, *panel_args, tau(r).astype(jnp.int32).reshape(1))

    cut = tiles_r * 2 // 3 if tiles_r % 3 == 0 else tiles_r
    pieces = [rows[:cut], rows[cut:]] if cut < tiles_r else [rows]
    mine, got = [], []
    for k, piece in enumerate(pieces):
        here, there = grid.spread(piece, k > 0, t, row_args[0])
        mine += here
        got += there
    info = jnp.stack([
        (r - c) % grid.n_col == 0, (r - c) // grid.n_col, tau(c), (r ^ c) & 1, r // grid.n_col,
    ]).astype(jnp.int32)
    out = trailing((x_rows, *row_args), mine, got, panel_args, info, step_tiles)
    return (
        low.reshape(tiles_r, 1, tile, PANEL),
        out.reshape(tiles_r, 1, tile, tiles_c, 1, tile),
    )


def solution(mesh):
    return jax.shard_map(
        local,
        mesh=mesh,
        in_specs=(P(None, "row", "col", None),),
        out_specs=(P(None, "row", None, None), P(None, "row", None, None, "col", None)),
        check_vma=False,
    )
```

```python
import functools

import jax
import jax.numpy as jnp
from jax import lax
from jax.experimental import pallas as pl
from jax.experimental.pallas import tpu as pltpu
from jax.sharding import PartitionSpec as P

F = 512
PANEL = 256
TILE = 128
RIDGE = 1.0
EPS = 1e-6

PV = (-2.265364170074463, -4.70527982711792, 7.536093711853027,
      0.7343835830688477, -1.7677195072174072, 0.3254770040512085)
QV = (1.8269329071044922, 3.1679749488830566, -4.871670722961426,
      0.626383364200592, 0.07849788665771484)
TINY = 1e-30
NT = (((1,), (1,)), ((), ()))
VMEM_LIMIT = 60 * 2**20


def dot_nt(a, b):
    return lax.dot_general(a, b, NT, preferred_element_type=jnp.float32)


def dot_hi(a, b, dims):
    return lax.dot_general(
        a, b, (dims, ((), ())), precision=lax.Precision.HIGHEST,
        preferred_element_type=jnp.float32,
    )


def horner(x, coefs):
    acc = coefs[-1]
    for c in coefs[-2::-1]:
        acc = acc * x + c
    return acc


def two_layers(rho):
    a = jnp.maximum(1.0 - rho, TINY)
    b = jnp.maximum(1.0 + rho, TINY)
    u = a * lax.rsqrt(a)
    v = b * lax.rsqrt(b)
    return horner(v, PV) + u * horner(v, QV)


def norm_rows(x):
    xf = x.astype(jnp.float32)
    return jnp.sum(xf * xf, axis=1, keepdims=True) / F


def norm_lanes(x):
    xf = x.astype(jnp.float32)
    sq = xf * xf
    hi = sq.astype(jnp.bfloat16)
    lo = (sq - hi.astype(jnp.float32)).astype(jnp.bfloat16)
    ones = jnp.ones((8, x.shape[1]), jnp.bfloat16)
    return (dot_nt(ones, hi) + dot_nt(ones, lo)) / F


def eye(n):
    return lax.broadcasted_iota(jnp.int32, (n, n), 0) == lax.broadcasted_iota(
        jnp.int32, (n, n), 1
    )


def eliminate(w_ref, t_ref):
    n = TILE
    sub = lax.broadcasted_iota(jnp.int32, (8, n), 0)
    for p in range(0, n, 8):
        a8 = w_ref[p : p + 8, :n]
        e8 = w_ref[p : p + 8, n:]
        cols = [jnp.broadcast_to(a8[:, p + k : p + k + 1], (8, n)) for k in range(8)]
        root = jnp.ones((8, n), jnp.float32)
        invs, ups = [], []
        for k in range(8):
            piv = cols[k][k : k + 1, :]
            inv = 1.0 / piv
            m = jnp.where(sub > k, cols[k], 0.0) * inv
            ak, ek = a8[k : k + 1, :], e8[k : k + 1, :]
            up = [cols[j][k : k + 1, :] for j in range(k + 1, 8)]
            for j in range(k + 1, 8):
                cols[j] = cols[j] - m * up[j - k - 1]
            a8 = a8 - m * ak
            e8 = e8 - m * ek
            root = jnp.where(sub == k, lax.rsqrt(piv), root)
            invs.append(inv)
            ups.append((ak, ek, up))
        t_ref[p : p + 8, :] = e8 * root
        for g in range(p + 8, n, 8):
            a = w_ref[g : g + 8, :n]
            e = w_ref[g : g + 8, n:]
            cs = [jnp.broadcast_to(a[:, p + k : p + k + 1], (8, n)) for k in range(8)]
            for k in range(8):
                ak, ek, up = ups[k]
                m = cs[k] * invs[k]
                for j in range(k + 1, 8):
                    cs[j] = cs[j] - m * up[j - k - 1]
                a = a - m * ak
                e = e - m * ek
            w_ref[g : g + 8, :n] = a
            w_ref[g : g + 8, n:] = e


def factor_kernel(x_ref, t_ref, sp_ref, bp_ref, k_ref, w_ref, t1_ref, t2_ref):
    x = x_ref[...]
    gq_l = norm_lanes(x)
    b_l = lax.rsqrt(gq_l + EPS)
    s_l = (gq_l + EPS) * b_l
    sp_ref[...] = s_l
    bp_ref[...] = b_l
    gq = norm_rows(x)
    s = jnp.sqrt(gq + EPS)
    rho = dot_nt(x, x) * ((1.0 / F) / s) * b_l[0:1, :]
    k = two_layers(rho) * (s * s_l[0:1, :])
    k_ref[...] = jnp.where(eye(PANEL), 3.0 * gq + (2.0 * EPS + RIDGE), k)
    h = PANEL // 2
    ident = jnp.where(eye(h), 1.0, 0.0)
    w_ref[:, :h] = k_ref[:h, :h]
    w_ref[:, h:] = ident
    eliminate(w_ref, t1_ref)
    t1 = t1_ref[...]
    l21 = dot_hi(k_ref[h:, :h], t1, ((1,), (1,)))
    w_ref[:, :h] = k_ref[h:, h:] - dot_hi(l21, l21, ((1,), (1,)))
    w_ref[:, h:] = ident
    eliminate(w_ref, t2_ref)
    t2 = t2_ref[...]
    t_ref[:h, :h] = t1
    t_ref[:h, h:] = jnp.zeros((h, h), jnp.float32)
    t_ref[h:, :h] = -dot_hi(t2, dot_hi(l21, t1, ((1,), (0,))), ((1,), (0,)))
    t_ref[h:, h:] = t2


def factor(points):
    full = jax.ShapeDtypeStruct((PANEL, PANEL), jnp.float32)
    vec = jax.ShapeDtypeStruct((8, PANEL), jnp.float32)
    return pl.pallas_call(
        factor_kernel,
        out_shape=[full, vec, vec],
        scratch_shapes=[
            pltpu.VMEM((PANEL, PANEL), jnp.float32),
            pltpu.VMEM((TILE, 2 * TILE), jnp.float32),
            pltpu.VMEM((TILE, TILE), jnp.float32),
            pltpu.VMEM((TILE, TILE), jnp.float32),
        ],
        compiler_params=pltpu.CompilerParams(vmem_limit_bytes=VMEM_LIMIT),
        cost_estimate=pl.CostEstimate(flops=12 * 10**9, bytes_accessed=10**6, transcendentals=0),
        name="factor",
    )(points)


def panel_block(x_ref, pts, sp, bp, k_ref):
    m = x_ref.shape[0]
    part = m // 2 if m % 32 == 0 else m
    norms = []
    for h in range(0, m, part):
        x = x_ref[h : h + part, :]
        gq = norm_rows(x)
        q = gq + EPS
        inv = lax.rsqrt(q)
        s = q * inv
        a = inv * (1.0 / F)
        k_ref[h : h + part, :] = dot_nt(x, pts)
        for g in range(0, part, 16):
            rows = slice(h + g, h + g + 16)
            rho = k_ref[rows, :] * a[g : g + 16, :] * bp
            k_ref[rows, :] = two_layers(rho) * (s[g : g + 16, :] * sp)
        norms.append((h, part, s, a, 3.0 * gq + (2.0 * EPS + RIDGE)))
    return norms


def set_diagonal(k_ref, diag, hit):
    for half in range(PANEL // TILE):
        cols = slice(half * TILE, (half + 1) * TILE)
        here = eye(TILE) & (hit == half)
        k_ref[:TILE, cols] = jnp.where(here, diag[:TILE, :], k_ref[:TILE, cols])


def split(low):
    hi = low.astype(jnp.bfloat16)
    return hi, (low - hi.astype(jnp.float32)).astype(jnp.bfloat16)


def panel_kernel(tau_ref, x_ref, pts_ref, t_ref, sp_ref, bp_ref,
                 l_ref, cat_ref, s_ref, a_ref, d_ref, k_ref):
    norms = panel_block(x_ref, pts_ref[...], sp_ref[0:1, :], bp_ref[0:1, :], k_ref)
    set_diagonal(k_ref, norms[0][4], jnp.where(pl.program_id(0) == 0, tau_ref[0], -1))
    for h, part, s, a, diag in norms:
        rows = slice(h, h + part)
        low = dot_hi(k_ref[rows, :], t_ref[...], ((1,), (1,)))
        hi, lo = split(low)
        l_ref[rows, :] = low
        cat_ref[rows, :PANEL] = hi
        cat_ref[rows, PANEL : 2 * PANEL] = hi
        cat_ref[rows, 2 * PANEL :] = lo
        s_ref[rows, :] = jnp.broadcast_to(s, (part, 128))
        a_ref[rows, :] = jnp.broadcast_to(a, (part, 128))
        left = diag - jnp.sum(low * low, axis=1, keepdims=True)
        d_ref[rows, :] = jnp.broadcast_to(left, (part, 128))


def pick(total, options):
    for o in options:
        if total % o == 0:
            return o
    return total


def panel_rows(x, points, t, sp, bp, tau):
    m = x.shape[0]
    block = pick(m, (512, 384, 256, 128))
    const = lambda shape: pl.BlockSpec(shape, lambda i: (0, 0))
    by_row = lambda width: pl.BlockSpec((block, width), lambda i: (i, 0))
    f32 = lambda *shape: jax.ShapeDtypeStruct(shape, jnp.float32)
    return pl.pallas_call(
        panel_kernel,
        grid=(m // block,),
        in_specs=[
            pl.BlockSpec(memory_space=pltpu.SMEM),
            by_row(F), const((PANEL, F)), const((PANEL, PANEL)),
            const((8, PANEL)), const((8, PANEL)),
        ],
        out_specs=[by_row(PANEL), by_row(3 * PANEL)] + [by_row(128)] * 3,
        out_shape=[f32(m, PANEL), jax.ShapeDtypeStruct((m, 3 * PANEL), jnp.bfloat16),
                   f32(m, 128), f32(m, 128), f32(m, 128)],
        scratch_shapes=[pltpu.VMEM((block, PANEL), jnp.float32)],
        compiler_params=pltpu.CompilerParams(vmem_limit_bytes=VMEM_LIMIT),
        cost_estimate=pl.CostEstimate(
            flops=12 * m * PANEL * (F + 6 * PANEL), bytes_accessed=m * 4096, transcendentals=0
        ),
        name="panel_rows",
    )(tau, x, points, t, sp, bp)


def trailing_kernel(rb, tb, blocks, steps, step_tiles, fold, arrays, info, *refs):
    mine, got, refs = refs[:arrays], refs[arrays : 2 * arrays], refs[2 * arrays :]
    pts, t_ref, sp_ref, bp_ref, xr, xr_next, lr, lr_next, sr, ar, dr = refs[:11]
    out, xc, lc, sc, bc, k_ref, ga, ma, gb, mb, sem = refs[-11:]
    if fold:
        out = out.reshape(rb * tb, TILE)
    q = pl.program_id(0)
    i, j = q // blocks, q % blocks
    cb = tb * TILE // 2
    per = cb // TILE

    size = k_ref.shape[0]

    def load(arrays):
        views = []
        for src in arrays:
            views += [src] if len(src.shape) == 3 else [src.at[e] for e in range(src.shape[0])]
        base = 0
        for k in range(0, len(views), step_tiles):
            for tile in range(views[k].shape[0]):
                for entry, src in enumerate(views[k : k + step_tiles]):
                    at = ((base + tile) * step_tiles + (info[4] ^ entry)) * TILE
                    to = xc.at[pl.ds(pl.multiple_of(at, TILE), TILE)]
                    pltpu.make_async_copy(src.at[tile], to, sem.at[at // size]).start()
            base += views[k].shape[0]

    def columns(b):
        rows = pl.ds(pl.multiple_of(b * size, size), size)
        pltpu.make_async_copy(xc.at[rows], xc.at[rows], sem.at[b]).wait()
        norms = panel_block(xc.at[rows], pts[...], sp_ref[0:1, :], bp_ref[0:1, :], k_ref)
        set_diagonal(k_ref, norms[0][4], jnp.where(b == 0, info[2], -1))
        for h, part, s, _, _ in norms:
            hi, lo = split(dot_hi(k_ref[h : h + part, :], t_ref[...], ((1,), (1,))))
            to = pl.ds(pl.multiple_of(b * size + h, part), part)
            lc[to, :PANEL] = hi
            lc[to, PANEL : 2 * PANEL] = lo
            lc[to, 2 * PANEL :] = hi
            for g in range(0, part, TILE):
                wide = jnp.broadcast_to(s[g : g + TILE, :], (TILE, TILE)).T[0:8, :]
                lanes = pl.ds(pl.multiple_of(b * size + h + g, TILE), TILE)
                sc[:, lanes] = wide
                bc[:, lanes] = 1.0 / wide

    def multiply(x, l, col, g, m):
        cols = pl.ds(pl.multiple_of(col, cb), cb)
        g[...] = dot_nt(x[...], xc[cols, :])
        m[...] = dot_nt(l[...], lc[cols, :])

    def finish(half, g, m):
        for tile in range(per):
            lanes = pl.ds(pl.multiple_of(j * (tb * TILE) + half * cb + tile * TILE, TILE), TILE)
            s_col = sc[0:1, lanes]
            b_col = bc[0:1, lanes]
            here = slice(tile * TILE, (tile + 1) * TILE)
            for k in range(0, rb, 16):
                rows = slice(k, k + 16)
                rho = g[rows, here] * ar[rows, :] * b_col
                val = two_layers(rho) * (sr[rows, :] * s_col) - m[rows, here]
                out[pl.ds(k * tb + half * per + tile, 16, stride=tb), :] = val

    @pl.when(q == 0)
    def _():
        @pl.when(info[3] == 0)
        def _():
            load(mine)

        @pl.when(info[3] != 0)
        def _():
            load(got)

        @pl.loop(0, xc.shape[0] // size)
        def _(b):
            columns(b)

        multiply(xr, lr, 0, ga, ma)

    multiply(xr, lr, j * (tb * TILE) + cb, gb, mb)
    finish(0, ga, ma)
    after = jnp.minimum(q + 1, steps - 1) % blocks
    multiply(xr_next, lr_next, after * (tb * TILE), ga, ma)
    finish(1, gb, mb)

    for tile in range(rb // TILE):
        col = (i * (rb // TILE) + tile) * step_tiles + info[1] - j * tb

        @pl.when((info[0] == 1) & (col >= 0) & (col < tb))
        def _():
            for k in range(0, TILE, 16):
                rows = slice(tile * TILE + k, tile * TILE + k + 16)
                same = lax.broadcasted_iota(jnp.int32, (16, TILE), 1) == (
                    lax.broadcasted_iota(jnp.int32, (16, TILE), 0) + k
                )
                at = pl.ds((tile * TILE + k) * tb + col, 16, stride=tb)
                out[at, :] = jnp.where(same, dr[rows, :], out[at, :])


def trailing(row_args, mine, got, panel_args, info, step_tiles):
    x_rows, cat_rows, s, a, d = row_args
    m = x_rows.shape[0]
    tiles_c = m // TILE * step_tiles
    n = tiles_c * TILE
    fold = tiles_c % 8 == 0
    tb = 8 if fold else tiles_c
    rb = pick(m, (512, 384, 256, 128))
    cb = tb * TILE // 2
    blocks = n // (tb * TILE)
    steps = m // rb * blocks
    size = pick(n, (512, 256))
    const = lambda shape: pl.BlockSpec(shape, lambda q: (0, 0))
    cur = lambda width: pl.BlockSpec((rb, width), lambda q: (q // blocks, 0))
    nxt = lambda width: pl.BlockSpec(
        (rb, width), lambda q: (jnp.minimum(q + 1, steps - 1) // blocks, 0)
    )
    hbm = pl.BlockSpec(memory_space=pl.ANY)
    if fold:
        shape = (m, tiles_c, TILE)
        spec = pl.BlockSpec((rb, tb, TILE), lambda q: (q // blocks, q % blocks, 0))
    else:
        shape = (m * tb, TILE)
        spec = pl.BlockSpec((rb * tb, TILE), lambda q: (q, 0))
    square = pltpu.VMEM((rb, cb), jnp.float32)
    return pl.pallas_call(
        functools.partial(
            trailing_kernel, rb, tb, blocks, steps, step_tiles, fold, len(mine)
        ),
        grid=(steps,),
        in_specs=[pl.BlockSpec(memory_space=pltpu.SMEM)] + [hbm] * (2 * len(mine)) + [
            const((PANEL, F)), const((PANEL, PANEL)), const((8, PANEL)), const((8, PANEL)),
            cur(F), nxt(F), cur(3 * PANEL), nxt(3 * PANEL), cur(128), cur(128), cur(128),
        ],
        out_specs=spec,
        out_shape=jax.ShapeDtypeStruct(shape, jnp.float32),
        scratch_shapes=[
            pltpu.VMEM((n, F), jnp.bfloat16),
            pltpu.VMEM((n, 3 * PANEL), jnp.bfloat16),
            pltpu.VMEM((8, n), jnp.float32),
            pltpu.VMEM((8, n), jnp.float32),
            pltpu.VMEM((size, PANEL), jnp.float32),
            square, square, square, square,
            pltpu.SemaphoreType.DMA((n // size,)),
        ],
        compiler_params=pltpu.CompilerParams(vmem_limit_bytes=VMEM_LIMIT),
        cost_estimate=pl.CostEstimate(
            flops=8 * m * n * (F + 3 * PANEL), bytes_accessed=m * n * 4, transcendentals=0
        ),
        name="trailing",
    )(info, *mine, *got, *panel_args, x_rows, x_rows, cat_rows, cat_rows, s, a, d)


class Grid:
    def __init__(self):
        self.n_row, self.n_col = lax.axis_size("row"), lax.axis_size("col")
        self.r, self.c = lax.axis_index("row"), lax.axis_index("col")
        self.low = self.n_col.bit_length() - 1
        self.high = self.n_row.bit_length() - 1

    def send(self, value, move):
        pairs = []
        for i in range(self.n_row):
            for j in range(self.n_col):
                to = move(i, j)
                if to is not None:
                    pairs.append((i * self.n_col + j, to[0] * self.n_col + to[1]))
        return lax.ppermute(value, ("row", "col"), pairs)

    def flip(self, value, bit, holds):
        return self.send(value, lambda i, j: (i ^ (1 << bit), j) if holds(i, j) else None)

    def turn(self, value, by, holds=lambda i, j: True):
        return self.send(value, lambda i, j: (i, (j + by) % self.n_col) if holds(i, j) else None)

    def in_order(self, own, before, after, across):
        parts = []
        for t in range(4):
            away = (t - self.c) % 4
            parts.append(jnp.where(away == 0, own, jnp.where(away == 3, before,
                         jnp.where(away == 1, after, across))))
        return jnp.concatenate(parts, axis=-2)

    def gather_rows(self, x, count):
        has = lambda i, j: i < count
        if self.n_col != 4:
            full = lax.all_gather(x, "col", axis=1, tiled=True)
            return full, self.share(full[0], count, None)
        before = self.turn(x, 1)
        after = self.turn(x, -1)
        across = self.turn(before, 1)
        tile = self.in_order(x[0], before[0], after[0], self.turn(before[0], 1, has))
        points = self.share(tile, count, across)
        return self.in_order(x, before, after, across), points

    def share(self, data, count, gate):
        bits = count.bit_length() - 1
        for bit in range(bits, self.high):
            got = self.flip(data, bit, lambda i, j: i >> bit == 0)
            data = jnp.where(self.r >> bit == 0, data, got)
            if bit == bits:
                data = tie(data, gate)
        data = data[None]
        for bit in range(bits):
            got = self.flip(data, bit, lambda i, j: True)
            first = (self.r >> bit) & 1 == 0
            data = jnp.concatenate([jnp.where(first, data, got), jnp.where(first, got, data)])
        return data

    def spread(self, data, high_first, second, last):
        mask = [self.n_col - 1]

        def copies(parts):
            for bit in range(self.low - 1, 0, -1):
                holds = lambda i, j: (i ^ j) & mask[0] == 0
                own = (self.r ^ self.c) & (1 << bit) == 0
                data = parts[0] if len(parts) == 1 else jnp.stack(parts)
                data = jnp.where(own, data, self.flip(data, bit, holds))
                parts = [data]
                mask[0] &= ~(1 << bit)
            return parts

        def swaps(parts):
            for bit in range(self.low, self.high):
                holds = lambda i, j: (i ^ j) & mask[0] == 0
                parts = parts + [self.flip(p, bit, holds) for p in parts]
            return parts

        steps = (swaps, copies) if high_first else (copies, swaps)
        parts = steps[0]([data])
        parts = steps[1]([tie(p, second) for p in parts])
        parts = [tie(p, last) for p in parts]
        return parts, [self.flip(p, 0, lambda i, j: (i ^ j) & 1 == 0) for p in parts]


def tie(value, earlier):
    return value if earlier is None else lax.optimization_barrier((value, earlier))[0]


def local(features):
    grid = Grid()
    r, c = grid.r, grid.c
    tiles_r, _, thin, width = features.shape
    step_tiles = grid.n_row // grid.n_col
    tiles_c = tiles_r * step_tiles
    tile = thin * grid.n_col

    rows, points = grid.gather_rows(features[:, 0], PANEL // tile)
    x_rows = rows.reshape(tiles_r * tile, width)
    points = points.reshape(PANEL, width)
    t, sp, bp = factor(points)
    panel_args = (points, t, sp, bp)
    tau = lambda i: jnp.where(i < PANEL // tile, i, -1)
    low, *row_args = panel_rows(x_rows, *panel_args, tau(r).astype(jnp.int32).reshape(1))

    cut = tiles_r * 3 // 4 if tiles_r % 12 == 0 else tiles_r
    pieces = [rows[:cut], rows[cut:]] if cut < tiles_r else [rows]
    mine, got = [], []
    for k, piece in enumerate(pieces):
        here, there = grid.spread(piece, k > 0, t, row_args[0])
        mine += here
        got += there
    info = jnp.stack([
        (r - c) % grid.n_col == 0, (r - c) // grid.n_col, tau(c), (r ^ c) & 1, r // grid.n_col,
    ]).astype(jnp.int32)
    out = trailing((x_rows, *row_args), mine, got, panel_args, info, step_tiles)
    return (
        low.reshape(tiles_r, 1, tile, PANEL),
        out.reshape(tiles_r, 1, tile, tiles_c, 1, tile),
    )


def solution(mesh):
    return jax.shard_map(
        local,
        mesh=mesh,
        in_specs=(P(None, "row", "col", None),),
        out_specs=(P(None, "row", None, None), P(None, "row", None, None, "col", None)),
        check_vma=False,
    )
```

```python
import functools

import jax
import jax.numpy as jnp
from jax import lax
from jax.experimental import pallas as pl
from jax.experimental.pallas import tpu as pltpu
from jax.sharding import PartitionSpec as P

F = 512
PANEL = 256
TILE = 128
RIDGE = 1.0
EPS = 1e-6

PV = (-2.265364170074463, -4.70527982711792, 7.536093711853027,
      0.7343835830688477, -1.7677195072174072, 0.3254770040512085)
QV = (1.8269329071044922, 3.1679749488830566, -4.871670722961426,
      0.626383364200592, 0.07849788665771484)
TINY = 1e-30
NT = (((1,), (1,)), ((), ()))
VMEM_LIMIT = 60 * 2**20


def dot_nt(a, b):
    return lax.dot_general(a, b, NT, preferred_element_type=jnp.float32)


def dot_hi(a, b, dims):
    return lax.dot_general(
        a, b, (dims, ((), ())), precision=lax.Precision.HIGHEST,
        preferred_element_type=jnp.float32,
    )


def horner(x, coefs):
    acc = coefs[-1]
    for c in coefs[-2::-1]:
        acc = acc * x + c
    return acc


def two_layers(rho):
    a = jnp.maximum(1.0 - rho, TINY)
    b = jnp.maximum(1.0 + rho, TINY)
    u = a * lax.rsqrt(a)
    v = b * lax.rsqrt(b)
    return horner(v, PV) + u * horner(v, QV)


def norm_rows(x):
    xf = x.astype(jnp.float32)
    return jnp.sum(xf * xf, axis=1, keepdims=True) / F


def norm_lanes(x):
    xf = x.astype(jnp.float32)
    sq = xf * xf
    hi = sq.astype(jnp.bfloat16)
    lo = (sq - hi.astype(jnp.float32)).astype(jnp.bfloat16)
    ones = jnp.ones((8, x.shape[1]), jnp.bfloat16)
    return (dot_nt(ones, hi) + dot_nt(ones, lo)) / F


def eye(n):
    return lax.broadcasted_iota(jnp.int32, (n, n), 0) == lax.broadcasted_iota(
        jnp.int32, (n, n), 1
    )


def eliminate(w_ref, t_ref):
    n = TILE
    sub = lax.broadcasted_iota(jnp.int32, (8, n), 0)
    for p in range(0, n, 8):
        a8 = w_ref[p : p + 8, :n]
        e8 = w_ref[p : p + 8, n:]
        cols = [jnp.broadcast_to(a8[:, p + k : p + k + 1], (8, n)) for k in range(8)]
        root = jnp.ones((8, n), jnp.float32)
        invs, ups = [], []
        for k in range(8):
            piv = cols[k][k : k + 1, :]
            inv = 1.0 / piv
            m = jnp.where(sub > k, cols[k], 0.0) * inv
            ak, ek = a8[k : k + 1, :], e8[k : k + 1, :]
            up = [cols[j][k : k + 1, :] for j in range(k + 1, 8)]
            for j in range(k + 1, 8):
                cols[j] = cols[j] - m * up[j - k - 1]
            a8 = a8 - m * ak
            e8 = e8 - m * ek
            root = jnp.where(sub == k, lax.rsqrt(piv), root)
            invs.append(inv)
            ups.append((ak, ek, up))
        t_ref[p : p + 8, :] = e8 * root
        for g in range(p + 8, n, 8):
            a = w_ref[g : g + 8, :n]
            e = w_ref[g : g + 8, n:]
            cs = [jnp.broadcast_to(a[:, p + k : p + k + 1], (8, n)) for k in range(8)]
            for k in range(8):
                ak, ek, up = ups[k]
                m = cs[k] * invs[k]
                for j in range(k + 1, 8):
                    cs[j] = cs[j] - m * up[j - k - 1]
                a = a - m * ak
                e = e - m * ek
            w_ref[g : g + 8, :n] = a
            w_ref[g : g + 8, n:] = e


def factor_kernel(x_ref, t_ref, sp_ref, bp_ref, k_ref, w_ref, t1_ref, t2_ref):
    x = x_ref[...]
    gq_l = norm_lanes(x)
    b_l = lax.rsqrt(gq_l + EPS)
    s_l = (gq_l + EPS) * b_l
    sp_ref[...] = s_l
    bp_ref[...] = b_l
    gq = norm_rows(x)
    s = jnp.sqrt(gq + EPS)
    rho = dot_nt(x, x) * ((1.0 / F) / s) * b_l[0:1, :]
    k = two_layers(rho) * (s * s_l[0:1, :])
    k_ref[...] = jnp.where(eye(PANEL), 3.0 * gq + (2.0 * EPS + RIDGE), k)
    h = PANEL // 2
    ident = jnp.where(eye(h), 1.0, 0.0)
    w_ref[:, :h] = k_ref[:h, :h]
    w_ref[:, h:] = ident
    eliminate(w_ref, t1_ref)
    t1 = t1_ref[...]
    l21 = dot_hi(k_ref[h:, :h], t1, ((1,), (1,)))
    w_ref[:, :h] = k_ref[h:, h:] - dot_hi(l21, l21, ((1,), (1,)))
    w_ref[:, h:] = ident
    eliminate(w_ref, t2_ref)
    t2 = t2_ref[...]
    t_ref[:h, :h] = t1
    t_ref[:h, h:] = jnp.zeros((h, h), jnp.float32)
    t_ref[h:, :h] = -dot_hi(t2, dot_hi(l21, t1, ((1,), (0,))), ((1,), (0,)))
    t_ref[h:, h:] = t2


def factor(points):
    full = jax.ShapeDtypeStruct((PANEL, PANEL), jnp.float32)
    vec = jax.ShapeDtypeStruct((8, PANEL), jnp.float32)
    return pl.pallas_call(
        factor_kernel,
        out_shape=[full, vec, vec],
        scratch_shapes=[
            pltpu.VMEM((PANEL, PANEL), jnp.float32),
            pltpu.VMEM((TILE, 2 * TILE), jnp.float32),
            pltpu.VMEM((TILE, TILE), jnp.float32),
            pltpu.VMEM((TILE, TILE), jnp.float32),
        ],
        compiler_params=pltpu.CompilerParams(vmem_limit_bytes=VMEM_LIMIT),
        cost_estimate=pl.CostEstimate(flops=12 * 10**9, bytes_accessed=10**6, transcendentals=0),
        name="factor",
    )(points)


def panel_block(x_ref, pts, sp, bp, k_ref):
    m = x_ref.shape[0]
    part = m // 2 if m % 32 == 0 else m
    norms = []
    for h in range(0, m, part):
        x = x_ref[h : h + part, :]
        gq = norm_rows(x)
        q = gq + EPS
        inv = lax.rsqrt(q)
        s = q * inv
        a = inv * (1.0 / F)
        k_ref[h : h + part, :] = dot_nt(x, pts)
        for g in range(0, part, 16):
            rows = slice(h + g, h + g + 16)
            rho = k_ref[rows, :] * a[g : g + 16, :] * bp
            k_ref[rows, :] = two_layers(rho) * (s[g : g + 16, :] * sp)
        norms.append((h, part, s, a, 3.0 * gq + (2.0 * EPS + RIDGE)))
    return norms


def set_diagonal(k_ref, diag, hit):
    for half in range(PANEL // TILE):
        cols = slice(half * TILE, (half + 1) * TILE)
        here = eye(TILE) & (hit == half)
        k_ref[:TILE, cols] = jnp.where(here, diag[:TILE, :], k_ref[:TILE, cols])


def split(low):
    hi = low.astype(jnp.bfloat16)
    return hi, (low - hi.astype(jnp.float32)).astype(jnp.bfloat16)


def panel_kernel(tau_ref, x_ref, pts_ref, t_ref, sp_ref, bp_ref,
                 l_ref, cat_ref, s_ref, a_ref, d_ref, k_ref):
    norms = panel_block(x_ref, pts_ref[...], sp_ref[0:1, :], bp_ref[0:1, :], k_ref)
    set_diagonal(k_ref, norms[0][4], jnp.where(pl.program_id(0) == 0, tau_ref[0], -1))
    for h, part, s, a, diag in norms:
        rows = slice(h, h + part)
        low = dot_hi(k_ref[rows, :], t_ref[...], ((1,), (1,)))
        hi, lo = split(low)
        l_ref[rows, :] = low
        cat_ref[rows, :PANEL] = hi
        cat_ref[rows, PANEL : 2 * PANEL] = hi
        cat_ref[rows, 2 * PANEL :] = lo
        s_ref[rows, :] = jnp.broadcast_to(s, (part, 128))
        a_ref[rows, :] = jnp.broadcast_to(a, (part, 128))
        left = diag - jnp.sum(low * low, axis=1, keepdims=True)
        d_ref[rows, :] = jnp.broadcast_to(left, (part, 128))


def pick(total, options):
    for o in options:
        if total % o == 0:
            return o
    return total


def panel_rows(x, points, t, sp, bp, tau):
    m = x.shape[0]
    block = pick(m, (512, 384, 256, 128))
    const = lambda shape: pl.BlockSpec(shape, lambda i: (0, 0))
    by_row = lambda width: pl.BlockSpec((block, width), lambda i: (i, 0))
    f32 = lambda *shape: jax.ShapeDtypeStruct(shape, jnp.float32)
    return pl.pallas_call(
        panel_kernel,
        grid=(m // block,),
        in_specs=[
            pl.BlockSpec(memory_space=pltpu.SMEM),
            by_row(F), const((PANEL, F)), const((PANEL, PANEL)),
            const((8, PANEL)), const((8, PANEL)),
        ],
        out_specs=[by_row(PANEL), by_row(3 * PANEL)] + [by_row(128)] * 3,
        out_shape=[f32(m, PANEL), jax.ShapeDtypeStruct((m, 3 * PANEL), jnp.bfloat16),
                   f32(m, 128), f32(m, 128), f32(m, 128)],
        scratch_shapes=[pltpu.VMEM((block, PANEL), jnp.float32)],
        compiler_params=pltpu.CompilerParams(vmem_limit_bytes=VMEM_LIMIT),
        cost_estimate=pl.CostEstimate(
            flops=12 * m * PANEL * (F + 6 * PANEL), bytes_accessed=m * 4096, transcendentals=0
        ),
        name="panel_rows",
    )(tau, x, points, t, sp, bp)


def trailing_kernel(rb, tb, blocks, steps, step_tiles, fold, arrays, info, *refs):
    mine, got, refs = refs[:arrays], refs[arrays : 2 * arrays], refs[2 * arrays :]
    pts, t_ref, sp_ref, bp_ref, xr, xr_next, lr, lr_next, sr, ar, dr = refs[:11]
    out, xc, lc, sc, bc, k_ref, ga, ma, gb, mb, sem = refs[-11:]
    if fold:
        out = out.reshape(rb * tb, TILE)
    q = pl.program_id(0)
    i, j = q // blocks, q % blocks
    cb = tb * TILE // 2
    per = cb // TILE

    size = k_ref.shape[0]

    def load(arrays):
        views = []
        for src in arrays:
            views += [src] if len(src.shape) == 3 else [src.at[e] for e in range(src.shape[0])]
        base = 0
        for k in range(0, len(views), step_tiles):
            for tile in range(views[k].shape[0]):
                for entry, src in enumerate(views[k : k + step_tiles]):
                    at = ((base + tile) * step_tiles + (info[4] ^ entry)) * TILE
                    to = xc.at[pl.ds(pl.multiple_of(at, TILE), TILE)]
                    pltpu.make_async_copy(src.at[tile], to, sem.at[at // size]).start()
            base += views[k].shape[0]

    def arrive(b):
        rows = xc.at[pl.ds(pl.multiple_of(b * size, size), size)]
        pltpu.make_async_copy(rows, rows, sem.at[b]).wait()

    def kernel_values(b):
        rows = pl.ds(pl.multiple_of(b * size, size), size)
        norms = panel_block(xc.at[rows], pts[...], sp_ref[0:1, :], bp_ref[0:1, :], k_ref)
        set_diagonal(k_ref, norms[0][4], jnp.where(b == 0, info[2], -1))
        for h, part, s, _, _ in norms:
            for g in range(0, part, TILE):
                wide = jnp.broadcast_to(s[g : g + TILE, :], (TILE, TILE)).T[0:8, :]
                lanes = pl.ds(pl.multiple_of(b * size + h + g, TILE), TILE)
                sc[:, lanes] = wide
                bc[:, lanes] = 1.0 / wide

    def lower_columns(b):
        part = size // 2
        for h in range(0, size, part):
            hi, lo = split(dot_hi(k_ref[h : h + part, :], t_ref[...], ((1,), (1,))))
            to = pl.ds(pl.multiple_of(b * size + h, part), part)
            lc[to, :PANEL] = hi
            lc[to, PANEL : 2 * PANEL] = lo
            lc[to, 2 * PANEL :] = hi

    def multiply(x, l, col, g, m):
        cols = pl.ds(pl.multiple_of(col, cb), cb)
        g[...] = dot_nt(x[...], xc[cols, :])
        m[...] = dot_nt(l[...], lc[cols, :])

    def finish(half, g, m):
        for tile in range(per):
            lanes = pl.ds(pl.multiple_of(j * (tb * TILE) + half * cb + tile * TILE, TILE), TILE)
            s_col = sc[0:1, lanes]
            b_col = bc[0:1, lanes]
            here = slice(tile * TILE, (tile + 1) * TILE)
            for k in range(0, rb, 16):
                rows = slice(k, k + 16)
                rho = g[rows, here] * ar[rows, :] * b_col
                val = two_layers(rho) * (sr[rows, :] * s_col) - m[rows, here]
                out[pl.ds(k * tb + half * per + tile, 16, stride=tb), :] = val

    @pl.when(q == 0)
    def _():
        @pl.when(info[3] == 0)
        def _():
            load(mine)

        @pl.when(info[3] != 0)
        def _():
            load(got)

        count = xc.shape[0] // size
        arrive(0)
        kernel_values(0)

        @pl.loop(0, count - 1)
        def _(b):
            arrive(b + 1)
            lower_columns(b)
            kernel_values(b + 1)

        lower_columns(count - 1)
        multiply(xr, lr, 0, ga, ma)

    multiply(xr, lr, j * (tb * TILE) + cb, gb, mb)
    finish(0, ga, ma)
    after = jnp.minimum(q + 1, steps - 1) % blocks
    multiply(xr_next, lr_next, after * (tb * TILE), ga, ma)
    finish(1, gb, mb)

    for tile in range(rb // TILE):
        col = (i * (rb // TILE) + tile) * step_tiles + info[1] - j * tb

        @pl.when((info[0] == 1) & (col >= 0) & (col < tb))
        def _():
            for k in range(0, TILE, 16):
                rows = slice(tile * TILE + k, tile * TILE + k + 16)
                same = lax.broadcasted_iota(jnp.int32, (16, TILE), 1) == (
                    lax.broadcasted_iota(jnp.int32, (16, TILE), 0) + k
                )
                at = pl.ds((tile * TILE + k) * tb + col, 16, stride=tb)
                out[at, :] = jnp.where(same, dr[rows, :], out[at, :])


def trailing(row_args, mine, got, panel_args, info, step_tiles):
    x_rows, cat_rows, s, a, d = row_args
    m = x_rows.shape[0]
    tiles_c = m // TILE * step_tiles
    n = tiles_c * TILE
    fold = tiles_c % 8 == 0
    tb = 8 if fold else tiles_c
    rb = pick(m, (512, 384, 256, 128))
    cb = tb * TILE // 2
    blocks = n // (tb * TILE)
    steps = m // rb * blocks
    size = pick(n, (512, 256))
    const = lambda shape: pl.BlockSpec(shape, lambda q: (0, 0))
    cur = lambda width: pl.BlockSpec((rb, width), lambda q: (q // blocks, 0))
    nxt = lambda width: pl.BlockSpec(
        (rb, width), lambda q: (jnp.minimum(q + 1, steps - 1) // blocks, 0)
    )
    hbm = pl.BlockSpec(memory_space=pl.ANY)
    if fold:
        shape = (m, tiles_c, TILE)
        spec = pl.BlockSpec((rb, tb, TILE), lambda q: (q // blocks, q % blocks, 0))
    else:
        shape = (m * tb, TILE)
        spec = pl.BlockSpec((rb * tb, TILE), lambda q: (q, 0))
    square = pltpu.VMEM((rb, cb), jnp.float32)
    return pl.pallas_call(
        functools.partial(
            trailing_kernel, rb, tb, blocks, steps, step_tiles, fold, len(mine)
        ),
        grid=(steps,),
        in_specs=[pl.BlockSpec(memory_space=pltpu.SMEM)] + [hbm] * (2 * len(mine)) + [
            const((PANEL, F)), const((PANEL, PANEL)), const((8, PANEL)), const((8, PANEL)),
            cur(F), nxt(F), cur(3 * PANEL), nxt(3 * PANEL), cur(128), cur(128), cur(128),
        ],
        out_specs=spec,
        out_shape=jax.ShapeDtypeStruct(shape, jnp.float32),
        scratch_shapes=[
            pltpu.VMEM((n, F), jnp.bfloat16),
            pltpu.VMEM((n, 3 * PANEL), jnp.bfloat16),
            pltpu.VMEM((8, n), jnp.float32),
            pltpu.VMEM((8, n), jnp.float32),
            pltpu.VMEM((size, PANEL), jnp.float32),
            square, square, square, square,
            pltpu.SemaphoreType.DMA((n // size,)),
        ],
        compiler_params=pltpu.CompilerParams(vmem_limit_bytes=VMEM_LIMIT),
        cost_estimate=pl.CostEstimate(
            flops=8 * m * n * (F + 3 * PANEL), bytes_accessed=m * n * 4, transcendentals=0
        ),
        name="trailing",
    )(info, *mine, *got, *panel_args, x_rows, x_rows, cat_rows, cat_rows, s, a, d)


class Grid:
    def __init__(self):
        self.n_row, self.n_col = lax.axis_size("row"), lax.axis_size("col")
        self.r, self.c = lax.axis_index("row"), lax.axis_index("col")
        self.low = self.n_col.bit_length() - 1
        self.high = self.n_row.bit_length() - 1

    def send(self, value, move):
        pairs = []
        for i in range(self.n_row):
            for j in range(self.n_col):
                to = move(i, j)
                if to is not None:
                    pairs.append((i * self.n_col + j, to[0] * self.n_col + to[1]))
        return lax.ppermute(value, ("row", "col"), pairs)

    def flip(self, value, bit, holds):
        return self.send(value, lambda i, j: (i ^ (1 << bit), j) if holds(i, j) else None)

    def turn(self, value, by, holds=lambda i, j: True):
        return self.send(value, lambda i, j: (i, (j + by) % self.n_col) if holds(i, j) else None)

    def in_order(self, own, before, after, across):
        parts = []
        for t in range(4):
            away = (t - self.c) % 4
            parts.append(jnp.where(away == 0, own, jnp.where(away == 3, before,
                         jnp.where(away == 1, after, across))))
        return jnp.concatenate(parts, axis=-2)

    def gather_rows(self, x, count):
        has = lambda i, j: i < count
        if self.n_col != 4:
            full = lax.all_gather(x, "col", axis=1, tiled=True)
            return full, self.share(full[0], count, None)
        before = self.turn(x, 1)
        after = self.turn(x, -1)
        across = self.turn(before, 1)
        tile = self.in_order(x[0], before[0], after[0], self.turn(before[0], 1, has))
        points = self.share(tile, count, across)
        return self.in_order(x, before, after, across), points

    def share(self, data, count, gate):
        bits = count.bit_length() - 1
        for bit in range(bits, self.high):
            got = self.flip(data, bit, lambda i, j: i >> bit == 0)
            data = jnp.where(self.r >> bit == 0, data, got)
            if bit == bits:
                data = tie(data, gate)
        data = data[None]
        for bit in range(bits):
            got = self.flip(data, bit, lambda i, j: True)
            first = (self.r >> bit) & 1 == 0
            data = jnp.concatenate([jnp.where(first, data, got), jnp.where(first, got, data)])
        return data

    def spread(self, data, high_first, second, last):
        mask = [self.n_col - 1]

        def copies(parts):
            for bit in range(self.low - 1, 0, -1):
                holds = lambda i, j: (i ^ j) & mask[0] == 0
                own = (self.r ^ self.c) & (1 << bit) == 0
                data = parts[0] if len(parts) == 1 else jnp.stack(parts)
                data = jnp.where(own, data, self.flip(data, bit, holds))
                parts = [data]
                mask[0] &= ~(1 << bit)
            return parts

        def swaps(parts):
            for bit in range(self.low, self.high):
                holds = lambda i, j: (i ^ j) & mask[0] == 0
                parts = parts + [self.flip(p, bit, holds) for p in parts]
            return parts

        steps = (swaps, copies) if high_first else (copies, swaps)
        parts = steps[0]([data])
        parts = steps[1]([tie(p, second) for p in parts])
        parts = [tie(p, last) for p in parts]
        return parts, [self.flip(p, 0, lambda i, j: (i ^ j) & 1 == 0) for p in parts]


def tie(value, earlier):
    return value if earlier is None else lax.optimization_barrier((value, earlier))[0]


def local(features):
    grid = Grid()
    r, c = grid.r, grid.c
    tiles_r, _, thin, width = features.shape
    step_tiles = grid.n_row // grid.n_col
    tiles_c = tiles_r * step_tiles
    tile = thin * grid.n_col

    rows, points = grid.gather_rows(features[:, 0], PANEL // tile)
    x_rows = rows.reshape(tiles_r * tile, width)
    points = points.reshape(PANEL, width)
    t, sp, bp = factor(points)
    panel_args = (points, t, sp, bp)
    tau = lambda i: jnp.where(i < PANEL // tile, i, -1)
    low, *row_args = panel_rows(x_rows, *panel_args, tau(r).astype(jnp.int32).reshape(1))

    cut = tiles_r * 3 // 4 if tiles_r % 12 == 0 else tiles_r
    pieces = [rows[:cut], rows[cut:]] if cut < tiles_r else [rows]
    mine, got = [], []
    for k, piece in enumerate(pieces):
        here, there = grid.spread(piece, k > 0, t, row_args[0])
        mine += here
        got += there
    info = jnp.stack([
        (r - c) % grid.n_col == 0, (r - c) // grid.n_col, tau(c), (r ^ c) & 1, r // grid.n_col,
    ]).astype(jnp.int32)
    out = trailing((x_rows, *row_args), mine, got, panel_args, info, step_tiles)
    return (
        low.reshape(tiles_r, 1, tile, PANEL),
        out.reshape(tiles_r, 1, tile, tiles_c, 1, tile),
    )


def solution(mesh):
    return jax.shard_map(
        local,
        mesh=mesh,
        in_specs=(P(None, "row", "col", None),),
        out_specs=(P(None, "row", None, None), P(None, "row", None, None, "col", None)),
        check_vma=False,
    )
```

```python
import functools

import jax
import jax.numpy as jnp
from jax import lax
from jax.experimental import pallas as pl
from jax.experimental.pallas import tpu as pltpu
from jax.sharding import PartitionSpec as P

F = 512
PANEL = 256
TILE = 128
RIDGE = 1.0
EPS = 1e-6

PV = (-2.265364170074463, -4.70527982711792, 7.536093711853027,
      0.7343835830688477, -1.7677195072174072, 0.3254770040512085)
QV = (1.8269329071044922, 3.1679749488830566, -4.871670722961426,
      0.626383364200592, 0.07849788665771484)
TINY = 1e-30
NT = (((1,), (1,)), ((), ()))
VMEM_LIMIT = 60 * 2**20


def dot_nt(a, b):
    return lax.dot_general(a, b, NT, preferred_element_type=jnp.float32)


def dot_hi(a, b, dims):
    return lax.dot_general(
        a, b, (dims, ((), ())), precision=lax.Precision.HIGHEST,
        preferred_element_type=jnp.float32,
    )


def horner(x, coefs):
    acc = coefs[-1]
    for c in coefs[-2::-1]:
        acc = acc * x + c
    return acc


def two_layers(rho):
    a = jnp.maximum(1.0 - rho, TINY)
    b = jnp.maximum(1.0 + rho, TINY)
    u = a * lax.rsqrt(a)
    v = b * lax.rsqrt(b)
    return horner(v, PV) + u * horner(v, QV)


def norm_rows(x):
    xf = x.astype(jnp.float32)
    return jnp.sum(xf * xf, axis=1, keepdims=True) / F


def norm_lanes(x):
    xf = x.astype(jnp.float32)
    sq = xf * xf
    hi = sq.astype(jnp.bfloat16)
    lo = (sq - hi.astype(jnp.float32)).astype(jnp.bfloat16)
    ones = jnp.ones((8, x.shape[1]), jnp.bfloat16)
    return (dot_nt(ones, hi) + dot_nt(ones, lo)) / F


def eye(n):
    return lax.broadcasted_iota(jnp.int32, (n, n), 0) == lax.broadcasted_iota(
        jnp.int32, (n, n), 1
    )


def eliminate(w_ref, t_ref):
    n = TILE
    sub = lax.broadcasted_iota(jnp.int32, (8, n), 0)
    for p in range(0, n, 8):
        a8 = w_ref[p : p + 8, :n]
        e8 = w_ref[p : p + 8, n:]
        cols = [jnp.broadcast_to(a8[:, p + k : p + k + 1], (8, n)) for k in range(8)]
        root = jnp.ones((8, n), jnp.float32)
        invs, ups = [], []
        for k in range(8):
            piv = cols[k][k : k + 1, :]
            inv = 1.0 / piv
            m = jnp.where(sub > k, cols[k], 0.0) * inv
            ak, ek = a8[k : k + 1, :], e8[k : k + 1, :]
            up = [cols[j][k : k + 1, :] for j in range(k + 1, 8)]
            for j in range(k + 1, 8):
                cols[j] = cols[j] - m * up[j - k - 1]
            a8 = a8 - m * ak
            e8 = e8 - m * ek
            root = jnp.where(sub == k, lax.rsqrt(piv), root)
            invs.append(inv)
            ups.append((ak, ek, up))
        t_ref[p : p + 8, :] = e8 * root
        for g in range(p + 8, n, 8):
            a = w_ref[g : g + 8, :n]
            e = w_ref[g : g + 8, n:]
            cs = [jnp.broadcast_to(a[:, p + k : p + k + 1], (8, n)) for k in range(8)]
            for k in range(8):
                ak, ek, up = ups[k]
                m = cs[k] * invs[k]
                for j in range(k + 1, 8):
                    cs[j] = cs[j] - m * up[j - k - 1]
                a = a - m * ak
                e = e - m * ek
            w_ref[g : g + 8, :n] = a
            w_ref[g : g + 8, n:] = e


def factor_kernel(odd_ref, own_ref, other_ref, t_ref, sp_ref, bp_ref, x_ref, k_ref, w_ref, t1_ref,
                  t2_ref):
    for odd in range(2):

        @pl.when(odd_ref[0] == odd)
        def _():
            x_ref[odd * TILE : (odd + 1) * TILE, :] = own_ref[...]
            x_ref[(1 - odd) * TILE : (2 - odd) * TILE, :] = other_ref[...]

    x = x_ref[...]
    gq_l = norm_lanes(x)
    b_l = lax.rsqrt(gq_l + EPS)
    s_l = (gq_l + EPS) * b_l
    sp_ref[...] = s_l
    bp_ref[...] = b_l
    gq = norm_rows(x)
    s = jnp.sqrt(gq + EPS)
    rho = dot_nt(x, x) * ((1.0 / F) / s) * b_l[0:1, :]
    k = two_layers(rho) * (s * s_l[0:1, :])
    k_ref[...] = jnp.where(eye(PANEL), 3.0 * gq + (2.0 * EPS + RIDGE), k)
    h = PANEL // 2
    ident = jnp.where(eye(h), 1.0, 0.0)
    w_ref[:, :h] = k_ref[:h, :h]
    w_ref[:, h:] = ident
    eliminate(w_ref, t1_ref)
    t1 = t1_ref[...]
    l21 = dot_hi(k_ref[h:, :h], t1, ((1,), (1,)))
    w_ref[:, :h] = k_ref[h:, h:] - dot_hi(l21, l21, ((1,), (1,)))
    w_ref[:, h:] = ident
    eliminate(w_ref, t2_ref)
    t2 = t2_ref[...]
    t_ref[:h, :h] = t1
    t_ref[:h, h:] = jnp.zeros((h, h), jnp.float32)
    t_ref[h:, :h] = -dot_hi(t2, dot_hi(l21, t1, ((1,), (0,))), ((1,), (0,)))
    t_ref[h:, h:] = t2


def factor(odd, own, other):
    full = jax.ShapeDtypeStruct((PANEL, PANEL), jnp.float32)
    vec = jax.ShapeDtypeStruct((8, PANEL), jnp.float32)
    return pl.pallas_call(
        factor_kernel,
        in_specs=[pl.BlockSpec(memory_space=pltpu.SMEM)] + [pl.BlockSpec(memory_space=pltpu.VMEM)] * 2,
        out_shape=[full, vec, vec, jax.ShapeDtypeStruct((PANEL, F), own.dtype)],
        scratch_shapes=[
            pltpu.VMEM((PANEL, PANEL), jnp.float32),
            pltpu.VMEM((TILE, 2 * TILE), jnp.float32),
            pltpu.VMEM((TILE, TILE), jnp.float32),
            pltpu.VMEM((TILE, TILE), jnp.float32),
        ],
        compiler_params=pltpu.CompilerParams(vmem_limit_bytes=VMEM_LIMIT),
        cost_estimate=pl.CostEstimate(flops=12 * 10**9, bytes_accessed=10**6, transcendentals=0),
        name="factor",
    )(odd, own, other)


def panel_block(x_ref, pts, sp, bp, k_ref):
    m = x_ref.shape[0]
    part = m // 2 if m % 32 == 0 else m
    norms = []
    for h in range(0, m, part):
        x = x_ref[h : h + part, :]
        gq = norm_rows(x)
        q = gq + EPS
        inv = lax.rsqrt(q)
        s = q * inv
        a = inv * (1.0 / F)
        k_ref[h : h + part, :] = dot_nt(x, pts)
        for g in range(0, part, 16):
            rows = slice(h + g, h + g + 16)
            rho = k_ref[rows, :] * a[g : g + 16, :] * bp
            k_ref[rows, :] = two_layers(rho) * (s[g : g + 16, :] * sp)
        norms.append((h, part, s, a, 3.0 * gq + (2.0 * EPS + RIDGE)))
    return norms


def set_diagonal(k_ref, diag, hit):
    for half in range(PANEL // TILE):
        cols = slice(half * TILE, (half + 1) * TILE)
        here = eye(TILE) & (hit == half)
        k_ref[:TILE, cols] = jnp.where(here, diag[:TILE, :], k_ref[:TILE, cols])


def split(low):
    hi = low.astype(jnp.bfloat16)
    return hi, (low - hi.astype(jnp.float32)).astype(jnp.bfloat16)


def panel_kernel(tau_ref, x_ref, pts_ref, t_ref, sp_ref, bp_ref,
                 l_ref, cat_ref, s_ref, a_ref, d_ref, k_ref):
    norms = panel_block(x_ref, pts_ref[...], sp_ref[0:1, :], bp_ref[0:1, :], k_ref)
    set_diagonal(k_ref, norms[0][4], jnp.where(pl.program_id(0) == 0, tau_ref[0], -1))
    for h, part, s, a, diag in norms:
        rows = slice(h, h + part)
        low = dot_hi(k_ref[rows, :], t_ref[...], ((1,), (1,)))
        hi, lo = split(low)
        l_ref[rows, :] = low
        cat_ref[rows, :PANEL] = hi
        cat_ref[rows, PANEL : 2 * PANEL] = hi
        cat_ref[rows, 2 * PANEL :] = lo
        s_ref[rows, :] = jnp.broadcast_to(s, (part, 128))
        a_ref[rows, :] = jnp.broadcast_to(a, (part, 128))
        left = diag - jnp.sum(low * low, axis=1, keepdims=True)
        d_ref[rows, :] = jnp.broadcast_to(left, (part, 128))


def pick(total, options):
    for o in options:
        if total % o == 0:
            return o
    return total


def panel_rows(x, points, t, sp, bp, tau):
    m = x.shape[0]
    block = pick(m, (512, 384, 256, 128))
    const = lambda shape: pl.BlockSpec(shape, lambda i: (0, 0))
    by_row = lambda width: pl.BlockSpec((block, width), lambda i: (i, 0))
    f32 = lambda *shape: jax.ShapeDtypeStruct(shape, jnp.float32)
    return pl.pallas_call(
        panel_kernel,
        grid=(m // block,),
        in_specs=[
            pl.BlockSpec(memory_space=pltpu.SMEM),
            by_row(F), const((PANEL, F)), const((PANEL, PANEL)),
            const((8, PANEL)), const((8, PANEL)),
        ],
        out_specs=[by_row(PANEL), by_row(3 * PANEL)] + [by_row(128)] * 3,
        out_shape=[f32(m, PANEL), jax.ShapeDtypeStruct((m, 3 * PANEL), jnp.bfloat16),
                   f32(m, 128), f32(m, 128), f32(m, 128)],
        scratch_shapes=[pltpu.VMEM((block, PANEL), jnp.float32)],
        compiler_params=pltpu.CompilerParams(vmem_limit_bytes=VMEM_LIMIT),
        cost_estimate=pl.CostEstimate(
            flops=12 * m * PANEL * (F + 6 * PANEL), bytes_accessed=m * 4096, transcendentals=0
        ),
        name="panel_rows",
    )(tau, x, points, t, sp, bp)


def trailing_kernel(rb, tb, blocks, steps, step_tiles, fold, arrays, info, *refs):
    mine, got, refs = refs[:arrays], refs[arrays : 2 * arrays], refs[2 * arrays :]
    pts, t_ref, sp_ref, bp_ref, xr, xr_next, lr, lr_next, sr, ar, dr = refs[:11]
    out, xc, lc, sc, bc, k_ref, ga, ma, gb, mb, sem = refs[-11:]
    if fold:
        out = out.reshape(rb * tb, TILE)
    q = pl.program_id(0)
    i, j = q // blocks, q % blocks
    cb = tb * TILE // 2
    per = cb // TILE

    size = k_ref.shape[0]

    def load(arrays):
        views = []
        for src in arrays:
            views += [src] if len(src.shape) == 3 else [src.at[e] for e in range(src.shape[0])]
        base = 0
        for k in range(0, len(views), step_tiles):
            for tile in range(views[k].shape[0]):
                for entry, src in enumerate(views[k : k + step_tiles]):
                    at = ((base + tile) * step_tiles + (info[4] ^ entry)) * TILE
                    to = xc.at[pl.ds(pl.multiple_of(at, TILE), TILE)]
                    pltpu.make_async_copy(src.at[tile], to, sem.at[at // size]).start()
            base += views[k].shape[0]

    def arrive(b):
        rows = xc.at[pl.ds(pl.multiple_of(b * size, size), size)]
        pltpu.make_async_copy(rows, rows, sem.at[b]).wait()

    def kernel_values(b):
        rows = pl.ds(pl.multiple_of(b * size, size), size)
        norms = panel_block(xc.at[rows], pts[...], sp_ref[0:1, :], bp_ref[0:1, :], k_ref)
        set_diagonal(k_ref, norms[0][4], jnp.where(b == 0, info[2], -1))
        for h, part, s, _, _ in norms:
            for g in range(0, part, TILE):
                wide = jnp.broadcast_to(s[g : g + TILE, :], (TILE, TILE)).T[0:8, :]
                lanes = pl.ds(pl.multiple_of(b * size + h + g, TILE), TILE)
                sc[:, lanes] = wide
                bc[:, lanes] = 1.0 / wide

    def lower_columns(b):
        part = size // 2
        for h in range(0, size, part):
            hi, lo = split(dot_hi(k_ref[h : h + part, :], t_ref[...], ((1,), (1,))))
            to = pl.ds(pl.multiple_of(b * size + h, part), part)
            lc[to, :PANEL] = hi
            lc[to, PANEL : 2 * PANEL] = lo
            lc[to, 2 * PANEL :] = hi

    def multiply(x, l, col, g, m):
        cols = pl.ds(pl.multiple_of(col, cb), cb)
        g[...] = dot_nt(x[...], xc[cols, :])
        m[...] = dot_nt(l[...], lc[cols, :])

    def finish(half, g, m):
        for tile in range(per):
            lanes = pl.ds(pl.multiple_of(j * (tb * TILE) + half * cb + tile * TILE, TILE), TILE)
            s_col = sc[0:1, lanes]
            b_col = bc[0:1, lanes]
            here = slice(tile * TILE, (tile + 1) * TILE)
            for k in range(0, rb, 16):
                rows = slice(k, k + 16)
                rho = g[rows, here] * ar[rows, :] * b_col
                val = two_layers(rho) * (sr[rows, :] * s_col) - m[rows, here]
                out[pl.ds(k * tb + half * per + tile, 16, stride=tb), :] = val

    @pl.when(q == 0)
    def _():
        @pl.when(info[3] == 0)
        def _():
            load(mine)

        @pl.when(info[3] != 0)
        def _():
            load(got)

        count = xc.shape[0] // size
        arrive(0)
        kernel_values(0)

        @pl.loop(0, count - 1)
        def _(b):
            arrive(b + 1)
            lower_columns(b)
            kernel_values(b + 1)

        lower_columns(count - 1)
        multiply(xr, lr, 0, ga, ma)

    multiply(xr, lr, j * (tb * TILE) + cb, gb, mb)
    finish(0, ga, ma)
    after = jnp.minimum(q + 1, steps - 1) % blocks
    multiply(xr_next, lr_next, after * (tb * TILE), ga, ma)
    finish(1, gb, mb)

    for tile in range(rb // TILE):
        col = (i * (rb // TILE) + tile) * step_tiles + info[1] - j * tb

        @pl.when((info[0] == 1) & (col >= 0) & (col < tb))
        def _():
            for k in range(0, TILE, 16):
                rows = slice(tile * TILE + k, tile * TILE + k + 16)
                same = lax.broadcasted_iota(jnp.int32, (16, TILE), 1) == (
                    lax.broadcasted_iota(jnp.int32, (16, TILE), 0) + k
                )
                at = pl.ds((tile * TILE + k) * tb + col, 16, stride=tb)
                out[at, :] = jnp.where(same, dr[rows, :], out[at, :])


def trailing(row_args, mine, got, panel_args, info, step_tiles):
    x_rows, cat_rows, s, a, d = row_args
    m = x_rows.shape[0]
    tiles_c = m // TILE * step_tiles
    n = tiles_c * TILE
    fold = tiles_c % 8 == 0
    tb = 8 if fold else tiles_c
    rb = pick(m, (512, 384, 256, 128))
    cb = tb * TILE // 2
    blocks = n // (tb * TILE)
    steps = m // rb * blocks
    size = pick(n, (512, 256))
    const = lambda shape: pl.BlockSpec(shape, lambda q: (0, 0))
    cur = lambda width: pl.BlockSpec((rb, width), lambda q: (q // blocks, 0))
    nxt = lambda width: pl.BlockSpec(
        (rb, width), lambda q: (jnp.minimum(q + 1, steps - 1) // blocks, 0)
    )
    hbm = pl.BlockSpec(memory_space=pl.ANY)
    if fold:
        shape = (m, tiles_c, TILE)
        spec = pl.BlockSpec((rb, tb, TILE), lambda q: (q // blocks, q % blocks, 0))
    else:
        shape = (m * tb, TILE)
        spec = pl.BlockSpec((rb * tb, TILE), lambda q: (q, 0))
    square = pltpu.VMEM((rb, cb), jnp.float32)
    return pl.pallas_call(
        functools.partial(
            trailing_kernel, rb, tb, blocks, steps, step_tiles, fold, len(mine)
        ),
        grid=(steps,),
        in_specs=[pl.BlockSpec(memory_space=pltpu.SMEM)] + [hbm] * (2 * len(mine)) + [
            const((PANEL, F)), const((PANEL, PANEL)), const((8, PANEL)), const((8, PANEL)),
            cur(F), nxt(F), cur(3 * PANEL), nxt(3 * PANEL), cur(128), cur(128), cur(128),
        ],
        out_specs=spec,
        out_shape=jax.ShapeDtypeStruct(shape, jnp.float32),
        scratch_shapes=[
            pltpu.VMEM((n, F), jnp.bfloat16),
            pltpu.VMEM((n, 3 * PANEL), jnp.bfloat16),
            pltpu.VMEM((8, n), jnp.float32),
            pltpu.VMEM((8, n), jnp.float32),
            pltpu.VMEM((size, PANEL), jnp.float32),
            square, square, square, square,
            pltpu.SemaphoreType.DMA((n // size,)),
        ],
        compiler_params=pltpu.CompilerParams(vmem_limit_bytes=VMEM_LIMIT),
        cost_estimate=pl.CostEstimate(
            flops=8 * m * n * (F + 3 * PANEL), bytes_accessed=m * n * 4, transcendentals=0
        ),
        name="trailing",
    )(info, *mine, *got, *panel_args, x_rows, x_rows, cat_rows, cat_rows, s, a, d)


class Grid:
    def __init__(self):
        self.n_row, self.n_col = lax.axis_size("row"), lax.axis_size("col")
        self.r, self.c = lax.axis_index("row"), lax.axis_index("col")
        self.low = self.n_col.bit_length() - 1
        self.high = self.n_row.bit_length() - 1

    def send(self, value, move):
        pairs = []
        for i in range(self.n_row):
            for j in range(self.n_col):
                to = move(i, j)
                if to is not None:
                    pairs.append((i * self.n_col + j, to[0] * self.n_col + to[1]))
        return lax.ppermute(value, ("row", "col"), pairs)

    def flip(self, value, bit, holds):
        return self.send(value, lambda i, j: (i ^ (1 << bit), j) if holds(i, j) else None)

    def turn(self, value, by, holds=lambda i, j: True):
        return self.send(value, lambda i, j: (i, (j + by) % self.n_col) if holds(i, j) else None)

    def in_order(self, own, before, after, across):
        parts = []
        for t in range(4):
            away = (t - self.c) % 4
            parts.append(jnp.where(away == 0, own, jnp.where(away == 3, before,
                         jnp.where(away == 1, after, across))))
        return jnp.concatenate(parts, axis=-2)

    def gather_rows(self, x, count):
        has = lambda i, j: i < count
        if self.n_col != 4:
            full = lax.all_gather(x, "col", axis=1, tiled=True)
            return full, self.share(full[0], count, None)
        before = self.turn(x, 1)
        after = self.turn(x, -1)
        across = self.turn(before, 1)
        tile = self.in_order(x[0], before[0], after[0], self.turn(before[0], 1, has))
        points = self.share(tile, count, across)
        return self.in_order(x, before, after, across), points

    def share(self, data, count, gate):
        bits = count.bit_length() - 1
        for bit in range(bits, self.high):
            got = self.flip(data, bit, lambda i, j: i >> bit == 0)
            data = jnp.where(self.r >> bit == 0, data, got)
            if bit == bits:
                data = tie(data, gate)
        return data, self.flip(data, 0, lambda i, j: True)

    def spread(self, data, high_first, second, last):
        mask = [self.n_col - 1]

        def copies(parts):
            for bit in range(self.low - 1, 0, -1):
                holds = lambda i, j: (i ^ j) & mask[0] == 0
                own = (self.r ^ self.c) & (1 << bit) == 0
                data = parts[0] if len(parts) == 1 else jnp.stack(parts)
                data = jnp.where(own, data, self.flip(data, bit, holds))
                parts = [data]
                mask[0] &= ~(1 << bit)
            return parts

        def swaps(parts):
            for bit in range(self.low, self.high):
                holds = lambda i, j: (i ^ j) & mask[0] == 0
                parts = parts + [self.flip(p, bit, holds) for p in parts]
            return parts

        steps = (swaps, copies) if high_first else (copies, swaps)
        parts = steps[0]([data])
        parts = steps[1]([tie(p, second) for p in parts])
        parts = [tie(p, last) for p in parts]
        return parts, [self.flip(p, 0, lambda i, j: (i ^ j) & 1 == 0) for p in parts]


def tie(value, earlier):
    return value if earlier is None else lax.optimization_barrier((value, earlier))[0]


def local(features):
    grid = Grid()
    r, c = grid.r, grid.c
    tiles_r, _, thin, width = features.shape
    step_tiles = grid.n_row // grid.n_col
    tiles_c = tiles_r * step_tiles
    tile = thin * grid.n_col

    rows, points = grid.gather_rows(features[:, 0], PANEL // tile)
    x_rows = rows.reshape(tiles_r * tile, width)
    t, sp, bp, points = factor((r & 1).astype(jnp.int32).reshape(1), *points)
    panel_args = (points, t, sp, bp)
    tau = lambda i: jnp.where(i < PANEL // tile, i, -1)
    low, *row_args = panel_rows(x_rows, *panel_args, tau(r).astype(jnp.int32).reshape(1))

    cut = tiles_r * 3 // 4 if tiles_r % 12 == 0 else tiles_r
    pieces = [rows[:cut], rows[cut:]] if cut < tiles_r else [rows]
    mine, got = [], []
    for k, piece in enumerate(pieces):
        here, there = grid.spread(piece, k > 0, t, row_args[0])
        mine += here
        got += there
    info = jnp.stack([
        (r - c) % grid.n_col == 0, (r - c) // grid.n_col, tau(c), (r ^ c) & 1, r // grid.n_col,
    ]).astype(jnp.int32)
    out = trailing((x_rows, *row_args), mine, got, panel_args, info, step_tiles)
    return (
        low.reshape(tiles_r, 1, tile, PANEL),
        out.reshape(tiles_r, 1, tile, tiles_c, 1, tile),
    )


def solution(mesh):
    return jax.shard_map(
        local,
        mesh=mesh,
        in_specs=(P(None, "row", "col", None),),
        out_specs=(P(None, "row", None, None), P(None, "row", None, None, "col", None)),
        check_vma=False,
    )
```
